512 devices in a mesh: dp: 32 (over y_hi, z, core), seq: 16 (over x, y_lo).
Axes of the slice: x: 4, y: 8 (y_hi: 2, y_lo: 4; y = y_hi * 4 + y_lo), z: 8, core: 2. Of those that a mesh axis runs over, the one named last changes fastest.
Arguments:
- out_grad: bfloat16 [32, 4096, 2240], P('dp', 'seq'), may hold values from -384 to 384
- out_weight: bfloat16 [1120, 2240], P('dp'), may hold values from -0.1875 to 0.1875
- queries: bfloat16 [32, 4096, 1120], P('dp', 'seq'), may hold values from -6 to 6
- keys: bfloat16 [32, 4096, 1120], P('dp', 'seq'), may hold values from -6 to 6
- values: bfloat16 [32, 4096, 1120], P('dp', 'seq'), may hold values from -6 to 6
- query_gain: float32 [1120], P('dp'), may hold values from 0.1 to 1.9
- key_norm_gain: float32 [1120], P('dp'), may hold values from 0.1 to 1.9
Outputs:
- query_grad: bfloat16 [32, 4096, 1120], P('dp', 'seq')
- key_gradient: bfloat16 [32, 4096, 1120], P('dp', 'seq')
- value_grad: bfloat16 [32, 4096, 1120], P('dp', 'seq')
- query_gain_grad: float32 [1120], P('dp')
- key_gain_grad: float32 [1120], P('dp')
The draws below stay inside these ranges and needn't reach their ends.
All inputs are finite; a program needn't handle non-finite values.
Results may differ from the reference program's by a relative error of at most 0.0085.
Values may be sent and summed in bfloat16 or wider, within the bound.
A program may use at most 64 MiB of HBM per device.

```python
import jax
import jax.numpy as jnp
from jax import lax

D = 2240
HEADS = 10
HEAD = 112
HE = 1120
TOKENS = 4096
CLIPS = 32


def steps_of(stream_key, dims, shards, least, top_value):
    factor_of, own = 1.0, jax.random.fold_in(stream_key, 6)
    for dim, parts in shards:
        heights = jnp.exp(jax.random.uniform(jax.random.fold_in(own, dim), (parts,), jnp.float32, least / len(shards), top_value / len(shards)))
        factor_of = factor_of * jnp.repeat(heights, dims[dim] // parts).reshape([-1 if axis == dim else 1 for axis in range(len(dims))])
    return factor_of


def centred(own_key, dims, spread, limit, split=(), kind=jnp.bfloat16):
    drawn = spread * jax.random.normal(own_key, dims, jnp.float32)
    if split:
        drawn = drawn * steps_of(own_key, dims, split, -0.22, 0.18)
    return jnp.clip(drawn, -limit, limit).astype(kind)


def setup_inputs(seed: int = 0) -> dict:
    splits = jax.random.split(jax.random.key(seed), 8)
    out_grad = centred(splits[0], (CLIPS, TOKENS, D), (TOKENS ** 0.5), 384.0, ((0, 32), (1, 16)))
    out_weight = centred(splits[1], (HE, D), HE ** -0.5, 0.1875, ((0, 32),))
    queries = centred(splits[2], (CLIPS, TOKENS, HE), 1.0, 6.0, ((0, 32), (1, 16)))
    keys = centred(splits[3], (CLIPS, TOKENS, HE), 1.0, 6.0, ((0, 32), (1, 16)))
    values = centred(splits[4], (CLIPS, TOKENS, HE), 1.0, 6.0, ((0, 32), (1, 16)))
    query_gain = jnp.clip(1.0 + 0.18 * jax.random.normal(splits[5], (HE,), jnp.float32), 0.1, 1.9)
    key_norm_gain = jnp.clip(1.0 + 0.18 * jax.random.normal(splits[6], (HE,), jnp.float32), 0.1, 1.9)
    return dict(out_grad=out_grad, out_weight=out_weight, queries=queries, keys=keys, values=values, query_gain=query_gain, key_norm_gain=key_norm_gain)


HIGH = lax.Precision.HIGHEST

def normalized_rows(raw, gain):
    rows = raw.shape[0]
    flat = raw.astype(jnp.float32).reshape(rows, HEADS, HEAD)
    scale = lax.rsqrt(lax.optimization_barrier(jnp.mean(flat * flat, axis=2, keepdims=True)) + 1e-06)
    return (flat, scale, gain.reshape(HEADS, HEAD)[None] * flat * scale)

def norm_backward(flat, scale, gain, grad):
    shaped = gain.reshape(HEADS, HEAD)[None] * grad
    inner = lax.optimization_barrier(jnp.mean(shaped * flat, axis=2, keepdims=True))
    return (scale * shaped - flat * scale ** 3 * inner, lax.optimization_barrier(jnp.sum(grad * flat * scale, axis=0)))

def one_clip(item):
    out_grad, queries, keys, values, out_weight, query_gain, key_norm_gain = item
    rows = queries.shape[0]
    qflat, qscale, qnorm = normalized_rows(queries, query_gain)
    flattened_keys, key_inverse_scale, key_rms_norm = normalized_rows(keys, key_norm_gain)
    phi_q = jnp.maximum(qnorm, 0.0).astype(jnp.bfloat16).astype(jnp.float32)
    phi_k = jnp.maximum(key_rms_norm, 0.0).astype(jnp.bfloat16).astype(jnp.float32)
    vals = values.astype(jnp.float32).reshape(rows, HEADS, HEAD)
    summary = jnp.einsum('thi,thj->hij', phi_k, vals, precision=HIGH)
    total = lax.optimization_barrier(jnp.sum(phi_k, axis=0))
    denom = jnp.einsum('thi,hi->th', phi_q, total, precision=HIGH)[:, :, None] + rows * 1.0
    attended = jnp.einsum('thi,hij->thj', phi_q, summary, precision=HIGH) / denom
    attn_grad = jnp.dot(out_grad, out_weight.T, preferred_element_type=jnp.float32).astype(jnp.bfloat16)
    attn_grad = attn_grad.astype(jnp.float32).reshape(rows, HEADS, HEAD)
    num_grad = attn_grad / denom
    denom_grad = -lax.optimization_barrier(jnp.sum(attn_grad * attended, axis=2, keepdims=True)) / denom
    summary_grad = jnp.einsum('thi,thj->hij', phi_q, num_grad, precision=HIGH)
    total_grad = lax.optimization_barrier(jnp.sum(denom_grad * phi_q, axis=0))
    phi_q_grad = jnp.einsum('thj,hij->thi', num_grad, summary, precision=HIGH) + denom_grad * total[None]
    phi_k_grad = jnp.einsum('thj,hij->thi', vals, summary_grad, precision=HIGH) + total_grad[None]
    value_grad = jnp.einsum('thi,hij->thj', phi_k, summary_grad, precision=HIGH)
    nq_grad = jnp.where(qflat > 0, phi_q_grad, 0.0)
    normed_key_gradient = jnp.where(flattened_keys > 0, phi_k_grad, 0.0)
    query_grad, query_gain_part = norm_backward(qflat, qscale, query_gain, nq_grad)
    key_gradient, key_gain_portion = norm_backward(flattened_keys, key_inverse_scale, key_norm_gain, normed_key_gradient)
    return (query_grad.reshape(rows, HE).astype(jnp.bfloat16), key_gradient.reshape(rows, HE).astype(jnp.bfloat16), value_grad.reshape(rows, HE).astype(jnp.bfloat16), query_gain_part.reshape(HE), key_gain_portion.reshape(HE))

def reference(out_grad, out_weight, queries, keys, values, query_gain, key_norm_gain):

    def step(index):
        return one_clip((out_grad[index], queries[index], keys[index], values[index], out_weight, query_gain, key_norm_gain))
    query_grad, key_gradient, value_grad, query_parts, key_parts = lax.map(step, jnp.arange(CLIPS, dtype=jnp.int32))
    return (query_grad, key_gradient, value_grad, lax.optimization_barrier(jnp.sum(query_parts, axis=0)), lax.optimization_barrier(jnp.sum(key_parts, axis=0)))
```

```python
import functools

import jax
import jax.numpy as jnp
from jax import lax
from jax.experimental import pallas as pl
from jax.experimental.pallas import tpu as pltpu
from jax.sharding import PartitionSpec as P

HEADS = 10
HEAD = 112
PAD = 128
ROWS = 256
WIDTH = HEADS * HEAD
MODEL = 2240
TOKENS = 4096
SEQ = 16
DP = 32
OWN = 35
HALF = 1152
CUT = 640
WIN = 80
PIECE = 80
BF = jnp.bfloat16
F32 = jnp.float32
MESH = pl.DeviceIdType.MESH


def first_tile(j):
    return (35 * j) // 8


OWNER = [max(j for j in range(SEQ) if first_tile(j) <= t) for t in range(70)]


def iota(shape, axis):
    return lax.broadcasted_iota(jnp.int32, shape, axis)


def dot_nt(a, b):
    return lax.dot_general(a, b, (((1,), (1,)), ((), ())), preferred_element_type=F32)


def dot_tn(a, b):
    return lax.dot_general(a, b, (((0,), (0,)), ((), ())), preferred_element_type=F32)


def dot_nn(a, b):
    return lax.dot_general(a, b, (((1,), (0,)), ((), ())), preferred_element_type=F32)


def kernel(
    og_in, w_in, q_in, k_in, v_in, gq_in, gk_in,
    qg_out, kg_out, vg_out, gqg_out, gkg_out,
    k_raw, v_raw, q_raw, w_raw, og, og_sib,
    kh, qh, vx, rkb, rqb, kp, ngx, qs,
    wpk, pair, wbuf, wh, att, att_send, gains,
    s_loc, s_recv, s_all, s_full,
    g_loc, g_recv, g_all, g_full,
    win_send, win_recv,
    in_sem, misc_s, misc_r, pair_s, pair_r, z_s, z_r, x_s, x_r,
    s_rs_s, s_rs_r, s_ag_s, s_ag_r, g_rs_s, g_rs_r, g_ag_s, g_ag_r, r_s, r_r,
):
    d = lax.axis_index("dp")
    s = lax.axis_index("seq")
    y = d // 16
    z = (d // 2) % 8
    c = d % 2
    p = (s // 4) % 2
    sib = (y * 16 + z * 2 + (1 - c), s)

    def remote(src, dst, ss, rs, dev):
        return pltpu.make_async_remote_copy(
            src_ref=src, dst_ref=dst, send_sem=ss, recv_sem=rs,
            device_id=dev, device_id_type=MESH,
        )

    ins = [
        pltpu.make_async_copy(a, b, in_sem.at[i])
        for i, (a, b) in enumerate(
            ((w_in, w_raw), (k_in, k_raw), (v_in, v_raw), (q_in, q_raw), (og_in, og))
        )
    ]
    for cp in ins:
        cp.start()
    bar = pltpu.get_barrier_semaphore()

    def greet_seq(o, u):
        pl.semaphore_signal(bar, inc=1, device_id=(d, (s + o) % SEQ), device_id_type=MESH)
        return u

    def greet_dp(o, u):
        pl.semaphore_signal(bar, inc=1, device_id=((d + o) % DP, s), device_id_type=MESH)
        return u

    lax.fori_loop(1, SEQ, greet_seq, 0)
    lax.fori_loop(1, DP, greet_dp, 0)

    ins[0].wait()
    wpk[...] = jnp.zeros_like(wpk)
    wpk[0:OWN, 0:MODEL] = w_raw[...]
    diag = iota((48, OWN), 0) == iota((48, OWN), 1)
    lane = iota((48, 64), 1)
    extra = jnp.zeros((48, 64), F32)
    for n, ref in enumerate((gq_in, gk_in)):
        col = jnp.sum(jnp.where(diag, jnp.broadcast_to(ref[...], (48, OWN)), 0.0), axis=1, keepdims=True)
        rest = col
        for m in range(3):
            part = rest.astype(BF).astype(F32)
            extra = jnp.where(lane == 3 * n + m, part, extra)
            rest = rest - part
    wpk[:, MODEL:] = extra.astype(BF)

    pl.semaphore_wait(bar, SEQ - 1 + DP - 1)

    far = remote(wpk, pair.at[c], pair_s.at[0], pair_r.at[c], ((1 - y) * 16 + z * 2 + y, s))
    near = remote(wpk, pair.at[c], pair_s.at[1], pair_r.at[c], sib)
    far.start()

    @pl.when(c != y)
    def _():
        near.start()

    @pl.when(c == y)
    def _():
        pair[c] = wpk[...]

    og_copy = remote(og_in, og_sib, misc_s.at[0], misc_r.at[0], sib)
    og_copy.start()

    kh[...] = jnp.zeros_like(kh)
    qh[...] = jnp.zeros_like(qh)
    vx[...] = jnp.where(iota(vx.shape, 2) == HEAD, 1.0, 0.0).astype(BF)
    s_full[...] = jnp.zeros_like(s_full)
    g_full[...] = jnp.zeros_like(g_full)
    ins[1].wait()
    ins[2].wait()
    for h in range(HEADS):
        cols = pl.ds(HEAD * h, HEAD)
        kh[h, :, 0:HEAD] = k_raw[:, cols]
        vx[h, :, 0:HEAD] = v_raw[:, cols]
    for h in range(HEADS):
        kf = kh[h].astype(F32)
        r = lax.rsqrt(jnp.sum(kf * kf, axis=1, keepdims=True) * (1.0 / HEAD) + 1e-06)
        rb = jnp.broadcast_to(r, (ROWS, PAD))
        rkb[h] = rb
        phi = jnp.maximum(kf * rb, 0.0).astype(BF)
        kp[h] = phi
        summ = dot_tn(phi, vx[h])
        s_loc[HEAD * h : HEAD * (h + 1), :] = summ[0:HEAD].astype(BF)

    def rs_send(loc, recv, ss, rs):
        def step(o, u):
            j = (s + o) % SEQ
            rows = pl.ds(pl.multiple_of(first_tile(j) * 16, 16), PIECE)
            remote(loc.at[rows], recv.at[o], ss.at[o], rs.at[o], (d, j)).start()
            return u

        lax.fori_loop(1, SEQ, step, 0)

    def rs_sum(loc, recv, ss, rs):
        acc = loc[pl.ds(pl.multiple_of(first_tile(s) * 16, 16), PIECE), :].astype(F32)

        def step(o, acc):
            remote(loc.at[pl.ds(0, PIECE)], recv.at[o], ss.at[o], rs.at[o], (d, s)).wait_recv()
            return acc + recv[o].astype(F32)

        return lax.fori_loop(1, SEQ, step, acc)

    def ag_send(all_, acc, ss, rs):
        all_[s] = acc.astype(BF)

        def step(o, u):
            remote(all_.at[s], all_.at[s], ss.at[o], rs.at[o], (d, (s + o) % SEQ)).start()
            return u

        lax.fori_loop(1, SEQ, step, 0)

    def ag_wait(all_, full, ss, rs):
        def step(o, u):
            j = (s + SEQ - o) % SEQ
            remote(all_.at[j], all_.at[j], ss.at[o], rs.at[o], (d, j)).wait_recv()
            return u

        lax.fori_loop(1, SEQ, step, 0)
        for t in range(70):
            j = OWNER[t]
            k = 16 * (t - first_tile(j))
            full[t // 7, 16 * (t % 7) : 16 * (t % 7) + 16, :] = all_[j, k : k + 16, :]

    rs_send(s_loc, s_recv, s_rs_s, s_rs_r)

    pair_wait = [remote(wpk, pair.at[i], pair_s.at[0], pair_r.at[i], sib) for i in range(2)]

    @pl.when((c != y) | (c == 1))
    def _():
        pair_wait[0].wait_recv()

    @pl.when((c != y) | (c == 0))
    def _():
        pair_wait[1].wait_recv()

    m = iota((WIN, 96), 1)
    to = (70 * z) % 16 + jnp.where(m < 48, m, m - 13)
    to = jnp.where(to >= WIN, to - WIN, to)
    good = (m < OWN) | ((m >= 48) & (m < 48 + OWN))
    place = jnp.where((iota((WIN, 96), 0) == to) & good, 1.0, 0.0).astype(BF)
    both = pair[...].reshape(96, 2 * HALF)
    window = dot_nn(place, both).astype(BF)
    wbuf[0, z] = window[:, :HALF]
    wbuf[1, z] = window[:, HALF:]

    up = (y * 16 + ((z + 1) % 8) * 2 + c, s)
    down = (y * 16 + ((z + 7) % 8) * 2 + c, s)
    right = (d, (s + 4) % SEQ)
    left = (d, (s + 12) % SEQ)
    part_a = pl.ds(0, CUT)
    part_b = pl.ds(CUT, HALF - CUT)

    def z_copy(way, k):
        b = (z - (k - 1) + 8) % 8 if way == 0 else (z + (k - 1)) % 8
        ref = wbuf.at[p, b]
        if k == 4:
            ref = wbuf.at[p, b, :, part_a if way == 0 else part_b]
        return remote(ref, ref, z_s.at[way, k - 1], z_r.at[way, k - 1], up if way == 0 else down)

    def x_copy(way, rel):
        b = (z + rel) % 8
        ref = wbuf.at[p, b, :, part_a if way == 0 else part_b]
        return remote(ref, ref, x_s.at[way, rel - 1], x_r.at[way, rel - 1], right if way == 0 else left)

    def x_wait(way, rel):
        b = (z + rel) % 8
        ref = wbuf.at[1 - p, b, :, part_a if way == 0 else part_b]
        remote(ref, ref, x_s.at[way, rel - 1], x_r.at[way, rel - 1], right).wait_recv()

    def z_step(k):
        z_copy(0, k).wait_recv()
        if k < 4:
            z_copy(0, k + 1).start()
            x_copy(0, 8 - k).start()
            x_copy(1, 8 - k).start()
        else:
            x_copy(0, 4).start()
        z_copy(1, k).wait_recv()
        if k < 4:
            z_copy(1, k + 1).start()
            x_copy(0, k).start()
            x_copy(1, k).start()
        else:
            x_copy(1, 4).start()

    z_copy(0, 1).start()
    z_copy(1, 1).start()

    ins[3].wait()
    for h in range(HEADS):
        qh[h, :, 0:HEAD] = q_raw[:, HEAD * h : HEAD * (h + 1)]
    for h in range(HEADS):
        qf = qh[h].astype(F32)
        r = lax.rsqrt(jnp.sum(qf * qf, axis=1, keepdims=True) * (1.0 / HEAD) + 1e-06)
        rqb[h] = jnp.broadcast_to(r, (ROWS, PAD))

    z_step(1)
    ag_send(s_all, rs_sum(s_loc, s_recv, s_rs_s, s_rs_r), s_ag_s, s_ag_r)
    z_step(2)
    z_step(3)
    ag_wait(s_all, s_full, s_ag_s, s_ag_r)
    z_step(4)
    for k in (1, 2, 3):
        for rel in (8 - k, k):
            x_wait(0, rel)
            x_wait(1, rel)
    x_wait(0, 4)
    x_wait(1, 4)

    row = iota((16, HALF), 0)
    for t in range(35):
        out = pl.ds(PAD * (t // 7) + 16 * (t % 7), 16)
        for e in range(2):
            tile = None
            for b in range(8):
                phase = (70 * b) % 16
                k = t - (70 * b) // 16
                over = phase + 70 - WIN
                if 0 <= k < 5:
                    piece = wbuf[e, b, 16 * k : 16 * k + 16, :]
                    if over > 0 and k == 0:
                        piece = jnp.where(row >= phase, piece, jnp.zeros_like(piece))
                elif k == 5 and over > 0:
                    piece = wbuf[e, b, 0:16, :]
                    piece = jnp.where(row < over, piece, jnp.zeros_like(piece))
                else:
                    continue
                tile = piece if tile is None else tile + piece
            wh[out, HALF * e : HALF * (e + 1)] = tile
    for h in range(5):
        wh[PAD * h + HEAD : PAD * (h + 1), :] = jnp.zeros((PAD - HEAD, 2 * HALF), BF)

    og_copy.wait_recv()
    ins[4].wait()
    sel_row = iota((16, 128), 0)
    sel_lane = iota((16, 128), 1)
    pick = ((sel_row == 0) & (sel_lane >= 64) & (sel_lane < 67)) | (
        (sel_row == 8) & (sel_lane >= 67) & (sel_lane < 70)
    )
    gains[c] = dot_nt(jnp.where(pick, 1.0, 0.0).astype(BF), wh[:, 2 * HALF - 128 :])
    gain_copy = remote(gains.at[c], gains.at[c], misc_s.at[1], misc_r.at[1], sib)
    gain_copy.start()
    att_send[...] = dot_nt(og_sib[...], wh[:, 0:MODEL]).astype(BF)
    att_copy = remote(att_send, att.at[c], misc_s.at[2], misc_r.at[2], sib)
    att_copy.start()
    att[c] = dot_nt(og[...], wh[:, 0:MODEL]).astype(BF)
    remote(gains.at[1 - c], gains.at[1 - c], misc_s.at[1], misc_r.at[1], sib).wait_recv()
    remote(att_send, att.at[1 - c], misc_s.at[2], misc_r.at[2], sib).wait_recv()

    def gain(n, h):
        return gains[h // 5, 8 * n : 8 * n + 1, PAD * (h % 5) : PAD * (h % 5 + 1)]

    tl = iota((ROWS, PAD), 1)
    for h in range(HEADS):
        gqk = gain(0, h) * gain(1, h)
        phi = jnp.maximum(qh[h].astype(F32) * rqb[h], 0.0)
        num = dot_nn((phi * gqk).astype(BF), s_full[h])
        inv = 1.0 / (num[:, HEAD : HEAD + 1] + float(TOKENS))
        ag = att[h // 5, :, PAD * (h % 5) : PAD * (h % 5 + 1)].astype(F32)
        ng = ag * inv
        dg = -jnp.sum(ng * num, axis=1, keepdims=True) * inv
        nx = jnp.where(tl == HEAD, dg, ng).astype(BF)
        ngx[h] = nx
        g_loc[HEAD * h : HEAD * (h + 1), :] = dot_tn(phi.astype(BF), nx)[0:HEAD].astype(BF)

    rs_send(g_loc, g_recv, g_rs_s, g_rs_r)

    def norm_back(raw, rb, grad):
        f = raw.astype(F32)
        a = jnp.where(f > 0, grad, 0.0)
        hat = f * rb
        mean = jnp.sum(a * hat, axis=1, keepdims=True) * (1.0 / HEAD)
        return (rb * (a - hat * mean)).astype(BF)

    for h in range(HEADS):
        gqk = gain(0, h) * gain(1, h)
        g = dot_nt(ngx[h], s_full[h]) * gqk
        qg_out[:, HEAD * h : HEAD * (h + 1)] = norm_back(qh[h], rqb[h], g)[:, 0:HEAD]

    ag_send(g_all, rs_sum(g_loc, g_recv, g_rs_s, g_rs_r), g_ag_s, g_ag_r)
    ag_wait(g_all, g_full, g_ag_s, g_ag_r)

    wins = jnp.zeros((DP, PAD), F32)
    for h in range(HEADS):
        rs_ = jnp.sum(s_full[h].astype(F32) * g_full[h].astype(F32), axis=1, keepdims=True)
        i_col = HEAD * h + iota((PAD, PAD), 0)
        block = (i_col * 1873) >> 16
        spot = (i_col - OWN * block == iota((PAD, PAD), 1)) & (iota((PAD, PAD), 0) < HEAD)
        spread = jnp.where(spot, jnp.broadcast_to(rs_, (PAD, PAD)), 0.0)
        i_row = HEAD * h + iota((DP, PAD), 1)
        which = jnp.where((i_row * 1873) >> 16 == iota((DP, PAD), 0), 1.0, 0.0).astype(BF)
        hi = spread.astype(BF)
        lo = (spread - hi.astype(F32)).astype(BF)
        wins = wins + dot_nn(which, hi) + dot_nn(which, lo)
    win_send[...] = wins.reshape(DP, 1, PAD)

    def win_step(o, u):
        e = (d + o) % DP
        remote(win_send.at[e], win_recv.at[o], r_s.at[o], r_r.at[o], (e, s)).start()
        return u

    lax.fori_loop(1, DP, win_step, 0)

    for h in range(HEADS):
        gqk = gain(0, h) * gain(1, h)
        g = dot_nt(vx[h], g_full[h]) * gqk
        cols = pl.ds(HEAD * h, HEAD)
        kg_out[:, cols] = norm_back(kh[h], rkb[h], g)[:, 0:HEAD]
        phi = (jnp.maximum(kh[h].astype(F32) * rkb[h], 0.0) * gqk).astype(BF)
        vg_out[:, cols] = dot_nn(phi, g_full[h])[:, 0:HEAD].astype(BF)

    def win_sum(o, acc):
        remote(win_send.at[0], win_recv.at[o], r_s.at[o], r_r.at[o], (d, s)).wait_recv()
        return acc + win_recv[o]

    total = lax.fori_loop(1, DP, win_sum, win_send[d])
    gqg_out[...] = total[:, 0:OWN] * gk_in[...]
    gkg_out[...] = total[:, 0:OWN] * gq_in[...]

    far.wait_send()

    @pl.when(c != y)
    def _():
        near.wait_send()

    og_copy.wait_send()
    gain_copy.wait_send()
    att_copy.wait_send()
    for way in range(2):
        for k in range(1, 5):
            z_copy(way, k).wait_send()
        for rel in range(1, 8):
            x_copy(way, rel).wait_send()

    def sent(o, u):
        for loc, all_, rs_, ag_ in (
            (s_loc, s_all, s_rs_s, s_ag_s),
            (g_loc, g_all, g_rs_s, g_ag_s),
        ):
            remote(loc.at[pl.ds(0, PIECE)], loc.at[pl.ds(0, PIECE)], rs_.at[o], rs_.at[o], (d, (s + o) % SEQ)).wait_send()
            remote(all_.at[s], all_.at[s], ag_.at[o], ag_.at[o], (d, (s + o) % SEQ)).wait_send()
        return u

    lax.fori_loop(1, SEQ, sent, 0)

    def win_sent(o, u):
        remote(win_send.at[0], win_recv.at[o], r_s.at[o], r_r.at[o], ((d + o) % DP, s)).wait_send()
        return u

    lax.fori_loop(1, DP, win_sent, 0)


def local(out_grad, out_weight, queries, keys, values, query_gain, key_norm_gain):
    V = pltpu.VMEM
    dma = pltpu.SemaphoreType.DMA
    any_, vm = pl.BlockSpec(memory_space=pl.ANY), pl.BlockSpec(memory_space=V)
    wide = jax.ShapeDtypeStruct((ROWS, WIDTH), BF)
    slim = jax.ShapeDtypeStruct((1, OWN), F32)
    head = (HEADS, ROWS, PAD)
    square = (HEADS, PAD, PAD)
    outs = pl.pallas_call(
        kernel,
        out_shape=(wide, wide, wide, slim, slim),
        in_specs=[any_] * 5 + [vm] * 2,
        out_specs=(vm,) * 5,
        scratch_shapes=[
            V((ROWS, WIDTH), BF), V((ROWS, WIDTH), BF), V((ROWS, WIDTH), BF),
            V((OWN, MODEL), BF), V((ROWS, MODEL), BF), V((ROWS, MODEL), BF),
            V(head, BF), V(head, BF), V(head, BF), V(head, F32), V(head, F32), V(head, BF), V(head, BF),
            V((8, 128), F32),
            V((48, 2 * HALF), BF), V((2, 48, 2 * HALF), BF),
            V((2, 8, WIN, HALF), BF), V((5 * PAD, 2 * HALF), BF),
            V((2, ROWS, 5 * PAD), BF), V((ROWS, 5 * PAD), BF), V((2, 16, 5 * PAD), F32),
            V((WIDTH, PAD), BF), V((SEQ, PIECE, PAD), BF), V((SEQ, PIECE, PAD), BF), V(square, BF),
            V((WIDTH, PAD), BF), V((SEQ, PIECE, PAD), BF), V((SEQ, PIECE, PAD), BF), V(square, BF),
            V((DP, 1, PAD), F32), V((DP, 1, PAD), F32),
            dma((5,)), dma((3,)), dma((3,)), dma((2,)), dma((2,)),
            dma((2, 4)), dma((2, 4)), dma((2, 7)), dma((2, 7)),
            *[dma((SEQ,))] * 8,
            dma((DP,)), dma((DP,)),
        ],
        compiler_params=pltpu.CompilerParams(
            collective_id=0, has_side_effects=True, vmem_limit_bytes=48 * 1024 * 1024
        ),
        cost_estimate=pl.CostEstimate(
            flops=2 * 512 * 2304 * 640, bytes_accessed=5_000_000, transcendentals=10_000
        ),
        name="attention_backward",
    )(
        out_grad[0], out_weight, queries[0], keys[0], values[0],
        query_gain.reshape(1, OWN), key_norm_gain.reshape(1, OWN),
    )
    qg, kg, vg, gq, gk = outs
    return qg[None], kg[None], vg[None], gq.reshape(OWN), gk.reshape(OWN)


def solution(mesh):
    placed = (
        P("dp", "seq", None),
        P("dp", None),
        P("dp", "seq", None),
        P("dp", "seq", None),
        P("dp", "seq", None),
        P("dp"),
        P("dp"),
    )
    return jax.shard_map(
        local,
        mesh=mesh,
        in_specs=placed,
        out_specs=(
            P("dp", "seq", None),
            P("dp", "seq", None),
            P("dp", "seq", None),
            P("dp"),
            P("dp"),
        ),
        check_vma=False,
    )
```

```python
import functools

import jax
import jax.numpy as jnp
from jax import lax
from jax.experimental import pallas as pl
from jax.experimental.pallas import tpu as pltpu
from jax.sharding import PartitionSpec as P

HEADS = 10
HEAD = 112
PAD = 128
ROWS = 256
WIDTH = HEADS * HEAD
MODEL = 2240
TOKENS = 4096
SEQ = 16
DP = 32
OWN = 35
HALF = 1152
CUT = 640
WIN = 80
PIECE = 80
BF = jnp.bfloat16
F32 = jnp.float32
MESH = pl.DeviceIdType.MESH


def first_tile(j):
    return (35 * j) // 8


OWNER = [max(j for j in range(SEQ) if first_tile(j) <= t) for t in range(70)]


def iota(shape, axis):
    return lax.broadcasted_iota(jnp.int32, shape, axis)


def dot_nt(a, b):
    return lax.dot_general(a, b, (((1,), (1,)), ((), ())), preferred_element_type=F32)


def dot_tn(a, b):
    return lax.dot_general(a, b, (((0,), (0,)), ((), ())), preferred_element_type=F32)


def dot_nn(a, b):
    return lax.dot_general(a, b, (((1,), (0,)), ((), ())), preferred_element_type=F32)


def kernel(
    og_in, w_in, q_in, k_in, v_in, gq_in, gk_in,
    qg_out, kg_out, vg_out, gqg_out, gkg_out,
    k_raw, q_raw, vx, w_raw, og, rk, rq, ngx,
    wpk, pair, wbuf, acc, gacc, att, att_send, gqk,
    s_loc, s_recv, s_all, s_full,
    g_loc, g_recv, g_all, g_full,
    s_own, win_send, win_recv, part_send, part_recv,
    in_sem, v_sem, misc_s, misc_r, pair_s, pair_r, z_s, z_r, x_s, x_r,
    s_rs_s, s_rs_r, s_ag_s, s_ag_r, g_rs_s, g_rs_r, g_ag_s, g_ag_r, r_s, r_r, t_s, t_r,
):
    d = lax.axis_index("dp")
    s = lax.axis_index("seq")
    y = d // 16
    z = (d // 2) % 8
    c = d % 2
    p = (s // 4) % 2
    sib = (y * 16 + z * 2 + (1 - c), s)
    up = (y * 16 + ((z + 1) % 8) * 2 + c, s)
    down = (y * 16 + ((z + 7) % 8) * 2 + c, s)
    right = (d, (s + 4) % SEQ)
    left = (d, (s + 12) % SEQ)
    far_dp = (1 - y) * 16 + z * 2
    far_seq = s - 2 * (s % 4) + 3

    def remote(src, dst, ss, rs, dev):
        return pltpu.make_async_remote_copy(
            src_ref=src, dst_ref=dst, send_sem=ss, recv_sem=rs,
            device_id=dev, device_id_type=MESH,
        )

    def head(h):
        return pl.ds(HEAD * h, HEAD)

    mine = pl.ds(0, ROWS)
    theirs = pl.ds(ROWS, ROWS)
    ins = [
        pltpu.make_async_copy(a, b, in_sem.at[i])
        for i, (a, b) in enumerate(
            ((w_in, w_raw), (k_in, k_raw), (q_in, q_raw), (og_in, og.at[pl.ds(0, MODEL), mine]))
        )
    ]
    ins_v = [
        pltpu.make_async_copy(v_in.at[head(h)], vx.at[h, pl.ds(0, HEAD)], v_sem.at[h])
        for h in range(HEADS)
    ]
    ins[0].start()
    ins[1].start()
    for cp in ins_v:
        cp.start()
    ins[2].start()
    ins[3].start()
    bar = pltpu.get_barrier_semaphore()

    def greet_seq(o, u):
        pl.semaphore_signal(bar, inc=1, device_id=(d, (s + o) % SEQ), device_id_type=MESH)
        return u

    def greet(dev):
        pl.semaphore_signal(bar, inc=1, device_id=dev, device_id_type=MESH)

    lax.fori_loop(1, SEQ, greet_seq, 0)
    greet(sib)
    greet(up)
    greet(down)

    @pl.when(c != y)
    def _():
        greet((far_dp, far_seq))
        greet((far_dp + 1, far_seq))

    ins[0].wait()
    wpk[...] = jnp.zeros_like(wpk)
    wpk[0:OWN, 0:MODEL] = w_raw[...]
    diag = iota((48, OWN), 0) == iota((48, OWN), 1)
    lane = iota((48, 64), 1)
    extra = jnp.zeros((48, 64), F32)
    for n, ref in enumerate((gq_in, gk_in)):
        col = jnp.sum(jnp.where(diag, jnp.broadcast_to(ref[...], (48, OWN)), 0.0), axis=1, keepdims=True)
        rest = col
        for m in range(3):
            part = rest.astype(BF).astype(F32)
            extra = jnp.where(lane == 3 * n + m, part, extra)
            rest = rest - part
    wpk[:, MODEL:] = extra.astype(BF)

    pl.semaphore_wait(bar, SEQ - 1 + 4)

    far = remote(wpk, pair.at[c], pair_s.at[0], pair_r.at[c], (far_dp + y, far_seq))
    near = remote(wpk, pair.at[c], pair_s.at[1], pair_r.at[c], sib)
    far.start()

    @pl.when(c != y)
    def _():
        near.start()

    @pl.when(c == y)
    def _():
        pair[c] = wpk[...]

    og_copy = remote(og_in, og.at[pl.ds(0, MODEL), theirs], misc_s.at[0], misc_r.at[0], sib)
    og_copy.start()

    ones = jnp.where(iota((16, ROWS), 0) == 0, 1.0, 0.0).astype(BF)
    og[MODEL:, :] = jnp.zeros((2 * HALF - MODEL, 2 * ROWS), BF)
    acc[...] = jnp.zeros_like(acc)
    gacc[...] = jnp.zeros_like(gacc)

    def inverse(f):
        return lax.rsqrt(jnp.sum(f * f, axis=0, keepdims=True) * (1.0 / HEAD) + 1e-06)

    ins[1].wait()
    for h in range(HEADS):
        kf = k_raw[head(h), :].astype(F32)
        r = inverse(kf)
        rk[h] = r
        phi = jnp.maximum(kf * r, 0.0).astype(BF)
        ins_v[h].wait()
        vx[h, HEAD:, :] = ones
        s_loc[head(h), :] = dot_nt(phi, vx[h]).astype(BF)

    def rs_send(loc, recv, ss, rs):
        def step(o, u):
            j = (s + o) % SEQ
            rows = pl.ds(pl.multiple_of(first_tile(j) * 16, 16), PIECE)
            remote(loc.at[rows], recv.at[o], ss.at[o], rs.at[o], (d, j)).start()
            return u

        lax.fori_loop(1, SEQ, step, 0)

    def rs_sum(loc, recv, ss, rs):
        total = loc[pl.ds(pl.multiple_of(first_tile(s) * 16, 16), PIECE), :].astype(F32)

        def step(o, total):
            remote(loc.at[pl.ds(0, PIECE)], recv.at[o], ss.at[o], rs.at[o], (d, s)).wait_recv()
            return total + recv[o].astype(F32)

        return lax.fori_loop(1, SEQ, step, total)

    def ag_send(all_, total, ss, rs):
        all_[s] = total.astype(BF)

        def step(o, u):
            remote(all_.at[s], all_.at[s], ss.at[o], rs.at[o], (d, (s + o) % SEQ)).start()
            return u

        lax.fori_loop(1, SEQ, step, 0)

    def ag_wait(all_, full, ss, rs):
        def step(o, u):
            j = (s + SEQ - o) % SEQ
            remote(all_.at[j], all_.at[j], ss.at[o], rs.at[o], (d, j)).wait_recv()
            return u

        lax.fori_loop(1, SEQ, step, 0)
        for j in range(SEQ):
            t = first_tile(j)
            n = 16 * (OWNER.count(j))
            full[16 * t : 16 * t + n, :] = all_[j, 0:n, :]

    rs_send(s_loc, s_recv, s_rs_s, s_rs_r)

    pair_wait = [remote(wpk, pair.at[i], pair_s.at[0], pair_r.at[i], sib) for i in range(2)]

    @pl.when((c != y) | (c == 1))
    def _():
        pair_wait[0].wait_recv()

    @pl.when((c != y) | (c == 0))
    def _():
        pair_wait[1].wait_recv()

    m = iota((WIN, 96), 1)
    to = (70 * z) % 16 + jnp.where(m < 48, m, m - 13)
    to = jnp.where(to >= WIN, to - WIN, to)
    good = (m < OWN) | ((m >= 48) & (m < 48 + OWN))
    place = jnp.where((iota((WIN, 96), 0) == to) & good, 1.0, 0.0).astype(BF)
    both = pair[...].reshape(96, 2 * HALF)
    window = dot_nn(place, both).astype(BF)
    wbuf[0, z] = window[:, :HALF]
    wbuf[1, z] = window[:, HALF:]

    part_a = pl.ds(0, CUT)
    part_b = pl.ds(CUT, HALF - CUT)

    def z_copy(way, k):
        b = (z - (k - 1) + 8) % 8 if way == 0 else (z + (k - 1)) % 8
        ref = wbuf.at[p, b]
        if k == 4:
            ref = wbuf.at[p, b, :, part_a if way == 0 else part_b]
        return remote(ref, ref, z_s.at[way, k - 1], z_r.at[way, k - 1], up if way == 0 else down)

    def x_copy(way, rel):
        b = (z + rel) % 8
        ref = wbuf.at[p, b, :, part_a if way == 0 else part_b]
        return remote(ref, ref, x_s.at[way, rel - 1], x_r.at[way, rel - 1], right if way == 0 else left)

    def x_wait(way, rel):
        b = (z + rel) % 8
        ref = wbuf.at[1 - p, b, :, part_a if way == 0 else part_b]
        remote(ref, ref, x_s.at[way, rel - 1], x_r.at[way, rel - 1], right).wait_recv()

    def z_step(k):
        z_copy(0, k).wait_recv()
        if k < 4:
            z_copy(0, k + 1).start()
            x_copy(0, 8 - k).start()
            x_copy(1, 8 - k).start()
        else:
            x_copy(0, 4).start()
        z_copy(1, k).wait_recv()
        if k < 4:
            z_copy(1, k + 1).start()
            x_copy(0, k).start()
            x_copy(1, k).start()
        else:
            x_copy(1, 4).start()

    z_copy(0, 1).start()
    z_copy(1, 1).start()

    row = iota((16, 1), 0)
    er = iota((128, 256), 0)
    el = iota((128, 256), 1)
    pick = ((er >= 64) & (er < 67) & (el < 128)) | ((er >= 67) & (er < 70) & (el >= 128))

    def add_rows(ref, b, res):
        start = pl.multiple_of(((70 * b) // 16) * 16, 16)
        phase = (70 * b) % 16
        over = phase + 70 - WIN
        ref[pl.ds(start, 16), :] += jnp.where(row >= phase, res[0:16], 0.0)
        ref[pl.ds(start + 16, WIN - 16), :] += res[16:]
        ref[pl.ds(start + WIN, 16), :] += jnp.where(row < over, res[0:16], 0.0)

    def product(e, b):
        rows = pl.ds(pl.multiple_of(e * HALF, 128), HALF)
        add_rows(acc, b, dot_nn(wbuf[e, b], og[rows, :]))
        spread = jnp.where(pick & (e == 1), 1.0, 0.0).astype(BF)
        add_rows(gacc, b, dot_nn(wbuf[e, b, :, HALF - 128 :], spread))

    ins[2].wait()
    for h in range(HEADS):
        rq[h] = inverse(q_raw[head(h), :].astype(F32))

    z_step(1)
    s_own[...] = rs_sum(s_loc, s_recv, s_rs_s, s_rs_r)
    ag_send(s_all, s_own[...], s_ag_s, s_ag_r)
    ins[3].wait()
    og_copy.wait_recv()
    product(p, z)
    product(1 - p, z)
    z_step(2)
    product(p, (z + 1) % 8)
    product(p, (z + 7) % 8)
    z_step(3)
    product(p, (z + 2) % 8)
    product(p, (z + 6) % 8)
    ag_wait(s_all, s_full, s_ag_s, s_ag_r)
    z_step(4)
    product(p, (z + 3) % 8)
    product(p, (z + 5) % 8)
    for rel in (1, 7, 2, 6, 3, 5):
        x_wait(0, rel)
        x_wait(1, rel)
        product(1 - p, (z + rel) % 8)
    product(p, (z + 4) % 8)
    x_wait(0, 4)
    x_wait(1, 4)
    product(1 - p, (z + 4) % 8)

    half_heads = 5 * HEAD
    att_send[...] = acc[0:half_heads, ROWS:].astype(BF)
    att_copy = remote(att_send, att.at[c], misc_s.at[2], misc_r.at[2], sib)
    att_copy.start()
    gqk[c] = gacc[0:half_heads, 0:128] * gacc[0:half_heads, 128:]
    gain_copy = remote(gqk.at[c], gqk.at[c], misc_s.at[1], misc_r.at[1], sib)
    gain_copy.start()
    att[c] = acc[0:half_heads, 0:ROWS].astype(BF)
    remote(gqk.at[1 - c], gqk.at[1 - c], misc_s.at[1], misc_r.at[1], sib).wait_recv()
    remote(att_send, att.at[1 - c], misc_s.at[2], misc_r.at[2], sib).wait_recv()

    def gain(h):
        g = gqk[h // 5, HEAD * (h % 5) : HEAD * (h % 5 + 1), :]
        return jnp.concatenate([g, g], axis=1)

    first = iota((16, ROWS), 0) == 0
    for h in range(HEADS):
        phi = jnp.maximum(q_raw[head(h), :].astype(F32) * rq[h], 0.0)
        num = dot_tn(s_full[head(h), :], (phi * gain(h)).astype(BF))
        inv = 1.0 / (num[HEAD : HEAD + 1] + float(TOKENS))
        ng = att[h // 5, HEAD * (h % 5) : HEAD * (h % 5 + 1), :].astype(F32) * inv
        dg = -jnp.sum(ng * num[0:HEAD], axis=0, keepdims=True) * inv
        ngx[h, 0:HEAD, :] = ng.astype(BF)
        ngx[h, HEAD:, :] = jnp.where(first, dg, 0.0).astype(BF)
        g_loc[head(h), :] = dot_nt(phi.astype(BF), ngx[h]).astype(BF)

    rs_send(g_loc, g_recv, g_rs_s, g_rs_r)

    def norm_back(raw, r, grad):
        f = raw.astype(F32)
        a = jnp.where(f > 0, grad, 0.0)
        hat = f * r
        mean = jnp.sum(a * hat, axis=0, keepdims=True) * (1.0 / HEAD)
        return (r * (a - hat * mean)).astype(BF)

    g_sum = rs_sum(g_loc, g_recv, g_rs_s, g_rs_r)
    ag_send(g_all, g_sum, g_ag_s, g_ag_r)
    sums = jnp.sum(g_sum * s_own[...], axis=1, keepdims=True)
    lanes = jnp.where(iota((PIECE, PAD), 0) == iota((PIECE, PAD), 1), jnp.broadcast_to(sums, (PIECE, PAD)), 0.0)
    win_send[...] = jnp.sum(lanes, axis=0, keepdims=True)

    def win_copy(o):
        return remote(win_send, win_recv.at[o], r_s.at[o], r_r.at[o], ((d + o) % DP, s))

    def win_step(o, u):
        win_copy(o).start()
        return u

    lax.fori_loop(1, DP, win_step, 0)

    for h in range(HEADS):
        g = dot_nn(s_full[head(h), :], ngx[h]) * gain(h)
        qg_out[head(h), :] = norm_back(q_raw[head(h), :], rq[h], g)

    def win_sum(o, total):
        win_copy(o).wait_recv()
        return total + win_recv[o]

    total = lax.fori_loop(1, DP, win_sum, win_send[...])
    own_first = first_tile(s)
    own_rows = 16 * (jnp.where(s == SEQ - 1, 70, first_tile(s + 1)) - own_first)
    at = iota((PAD, PAD), 1)
    spot = (at + 16 * own_first - OWN * d == iota((PAD, PAD), 0)) & (at < own_rows)
    spot = spot & (iota((PAD, PAD), 0) < OWN)
    col = jnp.sum(jnp.where(spot, jnp.broadcast_to(total, (PAD, PAD)), 0.0), axis=1, keepdims=True)
    across = jnp.where(iota((PAD, PAD), 0) == at, jnp.broadcast_to(col, (PAD, PAD)), 0.0)
    part_send[...] = jnp.sum(across, axis=0, keepdims=True)

    def part_copy(o):
        return remote(part_send, part_recv.at[o], t_s.at[o], t_r.at[o], (d, (s + o) % SEQ))

    def part_step(o, u):
        part_copy(o).start()
        return u

    lax.fori_loop(1, SEQ, part_step, 0)
    ag_wait(g_all, g_full, g_ag_s, g_ag_r)

    for h in range(HEADS):
        gg = gain(h)
        kf = k_raw[head(h), :].astype(F32)
        g = dot_nn(g_full[head(h), :], vx[h]) * gg
        kg_out[head(h), :] = norm_back(k_raw[head(h), :], rk[h], g)
        phi = (jnp.maximum(kf * rk[h], 0.0) * gg).astype(BF)
        vg_out[head(h), :] = dot_tn(g_full[head(h), :], phi)[0:HEAD].astype(BF)

    def part_sum(o, total):
        part_copy(o).wait_recv()
        return total + part_recv[o]

    total = lax.fori_loop(1, SEQ, part_sum, part_send[...])
    gqg_out[...] = total[:, 0:OWN] * gk_in[...]
    gkg_out[...] = total[:, 0:OWN] * gq_in[...]

    far.wait_send()

    @pl.when(c != y)
    def _():
        near.wait_send()

    og_copy.wait_send()
    gain_copy.wait_send()
    att_copy.wait_send()
    for way in range(2):
        for k in range(1, 5):
            z_copy(way, k).wait_send()
        for rel in range(1, 8):
            x_copy(way, rel).wait_send()

    def sent(o, u):
        for loc, all_, rs_, ag_ in (
            (s_loc, s_all, s_rs_s, s_ag_s),
            (g_loc, g_all, g_rs_s, g_ag_s),
        ):
            part = loc.at[pl.ds(0, PIECE)]
            remote(part, part, rs_.at[o], rs_.at[o], (d, (s + o) % SEQ)).wait_send()
            remote(all_.at[s], all_.at[s], ag_.at[o], ag_.at[o], (d, (s + o) % SEQ)).wait_send()
        return u

    lax.fori_loop(1, SEQ, sent, 0)

    def win_sent(o, u):
        win_copy(o).wait_send()
        return u

    lax.fori_loop(1, DP, win_sent, 0)

    def part_sent(o, u):
        part_copy(o).wait_send()
        return u

    lax.fori_loop(1, SEQ, part_sent, 0)


def local(out_grad, out_weight, queries, keys, values, query_gain, key_norm_gain):
    V = pltpu.VMEM
    dma = pltpu.SemaphoreType.DMA
    any_, vm = pl.BlockSpec(memory_space=pl.ANY), pl.BlockSpec(memory_space=V)
    wide = jax.ShapeDtypeStruct((WIDTH, ROWS), BF)
    slim = jax.ShapeDtypeStruct((1, OWN), F32)
    summed = [
        V((WIDTH, PAD), BF), V((SEQ, PIECE, PAD), BF), V((SEQ, PIECE, PAD), BF), V((WIDTH, PAD), BF),
    ]
    outs = pl.pallas_call(
        kernel,
        out_shape=(wide, wide, wide, slim, slim),
        in_specs=[any_] * 5 + [vm] * 2,
        out_specs=(vm,) * 5,
        scratch_shapes=[
            V((WIDTH, ROWS), BF), V((WIDTH, ROWS), BF), V((HEADS, PAD, ROWS), BF),
            V((OWN, MODEL), BF), V((2 * HALF, 2 * ROWS), BF),
            V((HEADS, 1, ROWS), F32), V((HEADS, 1, ROWS), F32), V((HEADS, PAD, ROWS), BF),
            V((48, 2 * HALF), BF), V((2, 48, 2 * HALF), BF), V((2, 8, WIN, HALF), BF),
            V((5 * HEAD + 32, 2 * ROWS), F32), V((5 * HEAD + 32, 256), F32),
            V((2, 5 * HEAD, ROWS), BF), V((5 * HEAD, ROWS), BF), V((2, 5 * HEAD, PAD), F32),
            *summed, *summed,
            V((PIECE, PAD), F32), V((1, PAD), F32), V((DP, 1, PAD), F32), V((1, PAD), F32), V((SEQ, 1, PAD), F32),
            dma((4,)), dma((HEADS,)), dma((3,)), dma((3,)), dma((2,)), dma((2,)),
            dma((2, 4)), dma((2, 4)), dma((2, 7)), dma((2, 7)),
            *[dma((SEQ,))] * 8,
            dma((DP,)), dma((DP,)), dma((SEQ,)), dma((SEQ,)),
        ],
        compiler_params=pltpu.CompilerParams(
            collective_id=0, has_side_effects=True, vmem_limit_bytes=63 * 1024 * 1024
        ),
        cost_estimate=pl.CostEstimate(
            flops=2 * 512 * 2304 * 640, bytes_accessed=5_000_000, transcendentals=10_000
        ),
        name="attention_backward",
    )(
        out_grad[0].T, out_weight, queries[0].T, keys[0].T, values[0].T,
        query_gain.reshape(1, OWN), key_norm_gain.reshape(1, OWN),
    )
    qg, kg, vg, gq, gk = outs
    return qg.T[None], kg.T[None], vg.T[None], gq.reshape(OWN), gk.reshape(OWN)


def solution(mesh):
    placed = (
        P("dp", "seq", None),
        P("dp", None),
        P("dp", "seq", None),
        P("dp", "seq", None),
        P("dp", "seq", None),
        P("dp"),
        P("dp"),
    )
    return jax.shard_map(
        local,
        mesh=mesh,
        in_specs=placed,
        out_specs=(
            P("dp", "seq", None),
            P("dp", "seq", None),
            P("dp", "seq", None),
            P("dp"),
            P("dp"),
        ),
        check_vma=False,
    )
```

```python
import functools

import jax
import jax.numpy as jnp
from jax import lax
from jax.experimental import pallas as pl
from jax.experimental.pallas import tpu as pltpu
from jax.sharding import PartitionSpec as P

HEADS = 10
HEAD = 112
PAD = 128
ROWS = 256
WIDTH = HEADS * HEAD
MODEL = 2240
TOKENS = 4096
SEQ = 16
DP = 32
OWN = 35
HALF = 1152
CUT = 384
PARTS = HALF // CUT
WIN = 80
PIECE = 80
GROUPS = ((0, 42, 3, 0), (672, 28, 2, 48))
BF = jnp.bfloat16
F32 = jnp.float32
MESH = pl.DeviceIdType.MESH


def first_tile(group, j):
    return (group[1] * j) // SEQ


OWNER = [
    [max(j for j in range(SEQ) if first_tile(g, j) <= t) for t in range(g[1])] for g in GROUPS
]


def iota(shape, axis):
    return lax.broadcasted_iota(jnp.int32, shape, axis)


def dot_nt(a, b):
    return lax.dot_general(a, b, (((1,), (1,)), ((), ())), preferred_element_type=F32)


def dot_tn(a, b):
    return lax.dot_general(a, b, (((0,), (0,)), ((), ())), preferred_element_type=F32)


def dot_nn(a, b):
    return lax.dot_general(a, b, (((1,), (0,)), ((), ())), preferred_element_type=F32)


def kernel(
    og_in, w_in, q_in, k_in, v_in, gq_in, gk_in,
    qg_out, kg_out, vg_out, gqg_out, gkg_out,
    k_raw, q_raw, vx, w_raw, og, rk, rq, ngx,
    wpk, pair, wbuf, acc, gacc, att, att_send, gqk,
    s_loc, s_recv, s_all, s_full,
    g_loc, g_recv, g_all, g_full,
    win_send, win_recv, part_send, part_recv,
    in_sem, v_sem, misc_s, misc_r, pair_s, pair_r, z_s, z_r, x_s, x_r,
    s_rs_s, s_rs_r, s_ag_s, s_ag_r, g_rs_s, g_rs_r, g_ag_s, g_ag_r, r_s, r_r, t_s, t_r,
):
    d = lax.axis_index("dp")
    s = lax.axis_index("seq")
    y = d // 16
    z = (d // 2) % 8
    c = d % 2
    p = (s // 4) % 2
    sib = (y * 16 + z * 2 + (1 - c), s)
    up = (y * 16 + ((z + 1) % 8) * 2 + c, s)
    down = (y * 16 + ((z + 7) % 8) * 2 + c, s)
    right = (d, (s + 4) % SEQ)
    left = (d, (s + 12) % SEQ)
    far_dp = (1 - y) * 16 + z * 2
    far_seq = s - 2 * (s % 4) + 3

    def remote(src, dst, ss, rs, dev):
        return pltpu.make_async_remote_copy(
            src_ref=src, dst_ref=dst, send_sem=ss, recv_sem=rs,
            device_id=dev, device_id_type=MESH,
        )

    def head(h):
        return pl.ds(HEAD * h, HEAD)

    mine = pl.ds(0, ROWS)
    theirs = pl.ds(ROWS, ROWS)
    ins = [
        pltpu.make_async_copy(a, b, in_sem.at[i])
        for i, (a, b) in enumerate(
            ((w_in, w_raw), (k_in, k_raw), (q_in, q_raw), (og_in, og.at[pl.ds(0, MODEL), mine]))
        )
    ]
    ins_v = [
        pltpu.make_async_copy(v_in.at[head(h)], vx.at[h, pl.ds(0, HEAD)], v_sem.at[h])
        for h in range(HEADS)
    ]
    ins[0].start()
    ins[1].start()
    for cp in ins_v:
        cp.start()
    ins[2].start()
    ins[3].start()
    bar = pltpu.get_barrier_semaphore()

    def greet_seq(o, u):
        pl.semaphore_signal(bar, inc=1, device_id=(d, (s + o) % SEQ), device_id_type=MESH)
        return u

    def greet(dev):
        pl.semaphore_signal(bar, inc=1, device_id=dev, device_id_type=MESH)

    lax.fori_loop(1, SEQ, greet_seq, 0)
    greet(sib)
    greet(up)
    greet(down)

    @pl.when(c != y)
    def _():
        greet((far_dp, far_seq))
        greet((far_dp + 1, far_seq))

    ins[0].wait()
    wpk[...] = jnp.zeros_like(wpk)
    wpk[0:OWN, 0:MODEL] = w_raw[...]
    diag = iota((48, OWN), 0) == iota((48, OWN), 1)
    lane = iota((48, 64), 1)
    extra = jnp.zeros((48, 64), F32)
    for n, ref in enumerate((gq_in, gk_in)):
        col = jnp.sum(jnp.where(diag, jnp.broadcast_to(ref[...], (48, OWN)), 0.0), axis=1, keepdims=True)
        rest = col
        for m in range(3):
            part = rest.astype(BF).astype(F32)
            extra = jnp.where(lane == 3 * n + m, part, extra)
            rest = rest - part
    wpk[:, MODEL:] = extra.astype(BF)

    ones = jnp.where(iota((16, ROWS), 0) == 0, 1.0, 0.0).astype(BF)
    og[MODEL:, :] = jnp.zeros((2 * HALF - MODEL, 2 * ROWS), BF)
    acc[...] = jnp.zeros_like(acc)
    gacc[...] = jnp.zeros_like(gacc)

    def inverse(f):
        return lax.rsqrt(jnp.sum(f * f, axis=0, keepdims=True) * (1.0 / HEAD) + 1e-06)

    def piece_rows(g):
        return pl.ds(g[3], 16 * g[2])

    def rs_copy(i, sums, o):
        g = GROUPS[i]
        j = (s + o) % SEQ
        rows = pl.ds(pl.multiple_of(g[0] + first_tile(g, j) * 16, 16), 16 * g[2])
        return remote(sums[0].at[rows], sums[1].at[o, piece_rows(g)], sums[4].at[i, o], sums[5].at[i, o], (d, j))

    def ag_copy(i, sums, o, j):
        piece = sums[2].at[j, piece_rows(GROUPS[i])]
        return remote(piece, piece, sums[6].at[i, o], sums[7].at[i, o], (d, (s + o) % SEQ))

    def rs_send(i, sums):
        def step(o, u):
            rs_copy(i, sums, o).start()
            return u

        lax.fori_loop(1, SEQ, step, 0)

    def rs_sum(i, sums):
        g = GROUPS[i]
        rows = pl.ds(pl.multiple_of(g[0] + first_tile(g, s) * 16, 16), 16 * g[2])

        def step(o, total):
            rs_copy(i, sums, o).wait_recv()
            return total + sums[1][o, g[3] : g[3] + 16 * g[2], :].astype(F32)

        return lax.fori_loop(1, SEQ, step, sums[0][rows, :].astype(F32))

    def ag_send(i, sums, total):
        g = GROUPS[i]
        sums[2][s, g[3] : g[3] + 16 * g[2], :] = total.astype(BF)

        def step(o, u):
            ag_copy(i, sums, o, s).start()
            return u

        lax.fori_loop(1, SEQ, step, 0)

    def ag_wait(i, sums):
        g = GROUPS[i]

        def step(o, u):
            ag_copy(i, sums, o, (s + SEQ - o) % SEQ).wait_recv()
            return u

        lax.fori_loop(1, SEQ, step, 0)
        for j in range(SEQ):
            row = g[0] + 16 * first_tile(g, j)
            n = 16 * OWNER[i].count(j)
            sums[3][row : row + n, :] = sums[2][j, g[3] : g[3] + n, :]

    s_sums = (s_loc, s_recv, s_all, s_full, s_rs_s, s_rs_r, s_ag_s, s_ag_r)
    g_sums = (g_loc, g_recv, g_all, g_full, g_rs_s, g_rs_r, g_ag_s, g_ag_r)

    def summary():
        ins[1].wait()
        for h in range(HEADS):
            ins_v[h].wait()
        vx[:, HEAD:, :] = jnp.broadcast_to(ones, (HEADS, PAD - HEAD, ROWS))
        for h in range(HEADS):
            kf = k_raw[head(h), :].astype(F32)
            r = inverse(kf)
            rk[h] = r
            phi = jnp.maximum(kf * r, 0.0).astype(BF)
            s_loc[head(h), :] = dot_nt(phi, vx[h]).astype(BF)

    early = z < 4

    @pl.when(early)
    def _():
        summary()

    pl.semaphore_wait(bar, SEQ - 1 + 4)

    far = remote(wpk, pair.at[c], pair_s.at[0], pair_r.at[c], (far_dp + y, far_seq))
    near = remote(wpk, pair.at[c], pair_s.at[1], pair_r.at[c], sib)
    far.start()

    @pl.when(c != y)
    def _():
        near.start()

    @pl.when(c == y)
    def _():
        pair[c] = wpk[...]

    og_copy = remote(og_in, og.at[pl.ds(0, MODEL), theirs], misc_s.at[0], misc_r.at[0], sib)
    og_copy.start()

    @pl.when(early)
    def _():
        rs_send(0, s_sums)
        rs_send(1, s_sums)

    pair_wait = [remote(wpk, pair.at[i], pair_s.at[0], pair_r.at[i], sib) for i in range(2)]

    @pl.when((c != y) | (c == 1))
    def _():
        pair_wait[0].wait_recv()

    @pl.when((c != y) | (c == 0))
    def _():
        pair_wait[1].wait_recv()

    m = iota((WIN, 96), 1)
    to = (70 * z) % 16 + jnp.where(m < 48, m, m - 13)
    to = jnp.where(to >= WIN, to - WIN, to)
    good = (m < OWN) | ((m >= 48) & (m < 48 + OWN))
    place = jnp.where((iota((WIN, 96), 0) == to) & good, 1.0, 0.0).astype(BF)
    both = pair[...].reshape(96, 2 * HALF)
    window = dot_nn(place, both).astype(BF)
    wbuf[0, z] = window[:, :HALF]
    wbuf[1, z] = window[:, HALF:]

    def part(e, b, q):
        return wbuf.at[e, b, :, pl.ds(CUT * q, CUT)]

    def z_copy(way, k, q):
        b = (z - (k - 1) + 8) % 8 if way == 0 else (z + (k - 1)) % 8
        ref = part(p, b, q)
        return remote(ref, ref, z_s.at[way, k - 1, q], z_r.at[way, k - 1, q], up if way == 0 else down)

    def x_copy(rel, q):
        ref = part(p, (z + rel) % 8, q)
        return remote(ref, ref, x_s.at[rel - 1, q], x_r.at[rel - 1, q], right if (q + rel) % 2 == 0 else left)

    def x_wait(rel):
        for q in range(PARTS):
            ref = part(1 - p, (z + rel) % 8, q)
            remote(ref, ref, x_s.at[rel - 1, q], x_r.at[rel - 1, q], right).wait_recv()

    def goes(way, k, q):
        return k < 4 or q % 2 == way

    def z_step(k):
        for q in range(PARTS):
            for way in range(2):
                if goes(way, k, q):
                    z_copy(way, k, q).wait_recv()
                    if k < 4 and goes(way, k + 1, q):
                        z_copy(way, k + 1, q).start()
                    x_copy(8 - k if way == 0 else k, q).start()

    for q in range(PARTS):
        z_copy(0, 1, q).start()
        z_copy(1, 1, q).start()

    @pl.when(z >= 4)
    def _():
        summary()
        rs_send(0, s_sums)
        rs_send(1, s_sums)

    row = iota((16, 1), 0)
    er = iota((128, 256), 0)
    el = iota((128, 256), 1)
    pick = ((er >= 64) & (er < 67) & (el < 128)) | ((er >= 67) & (er < 70) & (el >= 128))

    def add_rows(ref, b, res):
        start = pl.multiple_of(((70 * b) // 16) * 16, 16)
        phase = (70 * b) % 16
        over = phase + 70 - WIN
        ref[pl.ds(start, 16), :] += jnp.where(row >= phase, res[0:16], 0.0)
        ref[pl.ds(start + 16, WIN - 16), :] += res[16:]
        ref[pl.ds(start + WIN, 16), :] += jnp.where(row < over, res[0:16], 0.0)

    def product(e, b):
        rows = pl.ds(pl.multiple_of(e * HALF, 128), HALF)
        add_rows(acc, b, dot_nn(wbuf[e, b], og[rows, :]))
        spread = jnp.where(pick & (e == 1), 1.0, 0.0).astype(BF)
        add_rows(gacc, b, dot_nn(wbuf[e, b, :, HALF - 128 :], spread))

    ins[2].wait()
    for h in range(HEADS):
        rq[h] = inverse(q_raw[head(h), :].astype(F32))

    def spread_summary():
        for i in range(2):
            ag_send(i, s_sums, rs_sum(i, s_sums))

    @pl.when(early)
    def _():
        spread_summary()

    z_step(1)
    z_step(2)

    @pl.when(z >= 4)
    def _():
        spread_summary()

    ins[3].wait()
    og_copy.wait_recv()
    product(p, z)
    product(1 - p, z)
    z_step(3)
    for rel in (1, 7, 2, 6):
        product(p, (z + rel) % 8)
    z_step(4)
    ag_wait(0, s_sums)
    ag_wait(1, s_sums)
    for rel in (1, 7, 2, 6):
        x_wait(rel)
        product(1 - p, (z + rel) % 8)
    for rel in (3, 5, 4):
        product(p, (z + rel) % 8)
        x_wait(rel)
        product(1 - p, (z + rel) % 8)

    half_heads = 5 * HEAD
    att_send[...] = acc[0:half_heads, ROWS:].astype(BF)
    att_copy = remote(att_send, att.at[c], misc_s.at[2], misc_r.at[2], sib)
    att_copy.start()
    gqk[c] = gacc[0:half_heads, 0:128] * gacc[0:half_heads, 128:]
    gain_copy = remote(gqk.at[c], gqk.at[c], misc_s.at[1], misc_r.at[1], sib)
    gain_copy.start()
    att[c] = acc[0:half_heads, 0:ROWS].astype(BF)
    remote(gqk.at[1 - c], gqk.at[1 - c], misc_s.at[1], misc_r.at[1], sib).wait_recv()
    remote(att_send, att.at[1 - c], misc_s.at[2], misc_r.at[2], sib).wait_recv()

    def gain(h):
        g = gqk[h // 5, HEAD * (h % 5) : HEAD * (h % 5 + 1), :]
        return jnp.concatenate([g, g], axis=1)

    first = iota((16, ROWS), 0) == 0
    def grads_of(h):
        phi = jnp.maximum(q_raw[head(h), :].astype(F32) * rq[h], 0.0)
        num = dot_tn(s_full[head(h), :], (phi * gain(h)).astype(BF))
        inv = 1.0 / (num[HEAD : HEAD + 1] + float(TOKENS))
        ng = att[h // 5, HEAD * (h % 5) : HEAD * (h % 5 + 1), :].astype(F32) * inv
        dg = -jnp.sum(ng * num[0:HEAD], axis=0, keepdims=True) * inv
        ngx[h, 0:HEAD, :] = ng.astype(BF)
        ngx[h, HEAD:, :] = jnp.where(first, dg, 0.0).astype(BF)
        local = dot_nt(phi.astype(BF), ngx[h])
        g_loc[head(h), :] = local.astype(BF)
        sums = jnp.sum(local * s_full[head(h), :].astype(F32), axis=1, keepdims=True)
        i_col = HEAD * h + iota((HEAD, PAD), 0)
        spot = i_col - OWN * ((i_col * 1873) >> 16) == iota((HEAD, PAD), 1)
        spread = jnp.where(spot, jnp.broadcast_to(sums, (HEAD, PAD)), 0.0)
        i_row = HEAD * h + iota((DP, HEAD), 1)
        which = jnp.where((i_row * 1873) >> 16 == iota((DP, HEAD), 0), 1.0, 0.0).astype(BF)
        hi = spread.astype(BF)
        lo = (spread - hi.astype(F32)).astype(BF)
        return dot_nn(which, hi) + dot_nn(which, lo)

    wins = jnp.zeros((DP, PAD), F32)
    for h in range(0, 6):
        wins = wins + grads_of(h)
    rs_send(0, g_sums)
    for h in range(6, HEADS):
        wins = wins + grads_of(h)
    rs_send(1, g_sums)
    win_send[...] = wins.reshape(DP, 1, PAD)

    def win_copy(o):
        e = (d + o) % DP
        return remote(win_send.at[e], win_recv.at[o], r_s.at[o], r_r.at[o], (e, s))

    def win_step(o, u):
        win_copy(o).start()
        return u

    lax.fori_loop(1, DP, win_step, 0)

    def norm_back(raw, r, grad):
        f = raw.astype(F32)
        a = jnp.where(f > 0, grad, 0.0)
        hat = f * r
        mean = jnp.sum(a * hat, axis=0, keepdims=True) * (1.0 / HEAD)
        return (r * (a - hat * mean)).astype(BF)

    def query_grad(h):
        g = dot_nn(s_full[head(h), :], ngx[h]) * gain(h)
        qg_out[head(h), :] = norm_back(q_raw[head(h), :], rq[h], g)

    for h in range(HEADS):
        query_grad(h)

    for i in range(2):
        ag_send(i, g_sums, rs_sum(i, g_sums))

    def win_sum(o, total):
        win_copy(o).wait_recv()
        return total + win_recv[o]

    part_send[...] = lax.fori_loop(1, DP, win_sum, win_send[d])

    def part_copy(o):
        return remote(part_send, part_recv.at[o], t_s.at[o], t_r.at[o], (d, (s + o) % SEQ))

    def part_step(o, u):
        part_copy(o).start()
        return u

    lax.fori_loop(1, SEQ, part_step, 0)
    def key_grad(h):
        gg = gain(h)
        kf = k_raw[head(h), :].astype(F32)
        g = dot_nn(g_full[head(h), :], vx[h]) * gg
        kg_out[head(h), :] = norm_back(k_raw[head(h), :], rk[h], g)
        phi = (jnp.maximum(kf * rk[h], 0.0) * gg).astype(BF)
        vg_out[head(h), :] = dot_tn(g_full[head(h), :], phi)[0:HEAD].astype(BF)

    ag_wait(0, g_sums)
    for h in range(0, 6):
        key_grad(h)
    ag_wait(1, g_sums)
    for h in range(6, HEADS):
        key_grad(h)

    def part_sum(o, total):
        part_copy(o).wait_recv()
        return total + part_recv[o]

    total = lax.fori_loop(1, SEQ, part_sum, part_send[...])
    gqg_out[...] = total[:, 0:OWN] * gk_in[...]
    gkg_out[...] = total[:, 0:OWN] * gq_in[...]

    far.wait_send()

    @pl.when(c != y)
    def _():
        near.wait_send()

    og_copy.wait_send()
    gain_copy.wait_send()
    att_copy.wait_send()
    for q in range(PARTS):
        for way in range(2):
            for k in range(1, 5):
                if goes(way, k, q):
                    z_copy(way, k, q).wait_send()
        for rel in range(1, 8):
            x_copy(rel, q).wait_send()

    def sent(o, u):
        for i in range(2):
            for sums in (s_sums, g_sums):
                rs_copy(i, sums, o).wait_send()
                ag_copy(i, sums, o, s).wait_send()
        return u

    lax.fori_loop(1, SEQ, sent, 0)

    def win_sent(o, u):
        win_copy(o).wait_send()
        return u

    lax.fori_loop(1, DP, win_sent, 0)

    def part_sent(o, u):
        part_copy(o).wait_send()
        return u

    lax.fori_loop(1, SEQ, part_sent, 0)


def local(out_grad, out_weight, queries, keys, values, query_gain, key_norm_gain):
    V = pltpu.VMEM
    dma = pltpu.SemaphoreType.DMA
    any_, vm = pl.BlockSpec(memory_space=pl.ANY), pl.BlockSpec(memory_space=V)
    wide = jax.ShapeDtypeStruct((WIDTH, ROWS), BF)
    slim = jax.ShapeDtypeStruct((1, OWN), F32)
    summed = [
        V((WIDTH, PAD), BF), V((SEQ, PIECE, PAD), BF), V((SEQ, PIECE, PAD), BF), V((WIDTH, PAD), BF),
    ]
    outs = pl.pallas_call(
        kernel,
        out_shape=(wide, wide, wide, slim, slim),
        in_specs=[any_] * 5 + [vm] * 2,
        out_specs=(vm,) * 5,
        scratch_shapes=[
            V((WIDTH, ROWS), BF), V((WIDTH, ROWS), BF), V((HEADS, PAD, ROWS), BF),
            V((OWN, MODEL), BF), V((2 * HALF, 2 * ROWS), BF),
            V((HEADS, 1, ROWS), F32), V((HEADS, 1, ROWS), F32), V((HEADS, PAD, ROWS), BF),
            V((48, 2 * HALF), BF), V((2, 48, 2 * HALF), BF), V((2, 8, WIN, HALF), BF),
            V((5 * HEAD + 32, 2 * ROWS), F32), V((5 * HEAD + 32, 256), F32),
            V((2, 5 * HEAD, ROWS), BF), V((5 * HEAD, ROWS), BF), V((2, 5 * HEAD, PAD), F32),
            *summed, *summed,
            V((DP, 1, PAD), F32), V((DP, 1, PAD), F32), V((1, PAD), F32), V((SEQ, 1, PAD), F32),
            dma((4,)), dma((HEADS,)), dma((3,)), dma((3,)), dma((2,)), dma((2,)),
            dma((2, 4, PARTS)), dma((2, 4, PARTS)), dma((7, PARTS)), dma((7, PARTS)),
            *[dma((2, SEQ))] * 8,
            dma((DP,)), dma((DP,)), dma((SEQ,)), dma((SEQ,)),
        ],
        compiler_params=pltpu.CompilerParams(
            collective_id=0, has_side_effects=True, vmem_limit_bytes=63 * 1024 * 1024
        ),
        cost_estimate=pl.CostEstimate(
            flops=2 * 512 * 2304 * 640, bytes_accessed=5_000_000, transcendentals=10_000
        ),
        name="attention_backward",
    )(
        out_grad[0].T, out_weight, queries[0].T, keys[0].T, values[0].T,
        query_gain.reshape(1, OWN), key_norm_gain.reshape(1, OWN),
    )
    qg, kg, vg, gq, gk = outs
    return qg.T[None], kg.T[None], vg.T[None], gq.reshape(OWN), gk.reshape(OWN)


def solution(mesh):
    placed = (
        P("dp", "seq", None),
        P("dp", None),
        P("dp", "seq", None),
        P("dp", "seq", None),
        P("dp", "seq", None),
        P("dp"),
        P("dp"),
    )
    return jax.shard_map(
        local,
        mesh=mesh,
        in_specs=placed,
        out_specs=(
            P("dp", "seq", None),
            P("dp", "seq", None),
            P("dp", "seq", None),
            P("dp"),
            P("dp"),
        ),
        check_vma=False,
    )
```

```python
import functools

import jax
import jax.numpy as jnp
from jax import lax
from jax.experimental import pallas as pl
from jax.experimental.pallas import tpu as pltpu
from jax.sharding import PartitionSpec as P

HEADS = 10
HEAD = 112
PAD = 128
ROWS = 256
WIDTH = HEADS * HEAD
MODEL = 2240
TOKENS = 4096
SEQ = 16
DP = 32
OWN = 35
HALF = 1152
CUT = 384
PARTS = HALF // CUT
WIN = 80
PIECE = 80
GROUPS = ((4, 28, 2, 0), (6, 42, 3, 32))
BF = jnp.bfloat16
F32 = jnp.float32
MESH = pl.DeviceIdType.MESH


def first_tile(group, j):
    return (group[1] * j) // SEQ


OWNER = [
    [max(j for j in range(SEQ) if first_tile(g, j) <= t) for t in range(g[1])] for g in GROUPS
]


def iota(shape, axis):
    return lax.broadcasted_iota(jnp.int32, shape, axis)


def dot_nt(a, b):
    return lax.dot_general(a, b, (((1,), (1,)), ((), ())), preferred_element_type=F32)


def dot_tn(a, b):
    return lax.dot_general(a, b, (((0,), (0,)), ((), ())), preferred_element_type=F32)


def dot_nn(a, b):
    return lax.dot_general(a, b, (((1,), (0,)), ((), ())), preferred_element_type=F32)


def kernel(
    og_in, w_in, q_in, k_in, v_in, gq_in, gk_in,
    qg_out, kg_out, vg_out, total_out,
    gq_raw, gk_raw, qg, kg, vg, k_raw, q_raw, vx, w_raw, og, rk, rq, ngx,
    pair, wbuf, acc, gacc, att, att_send, gqk,
    s_loc, s_recv, s_all, s_full,
    g_loc, g_recv, g_all, g_full,
    win_send, win_recv, part_send, part_recv,
    in_sem, out_sem, v_sem, misc_s, misc_r, pair_s, pair_r, z_s, z_r, x_s, x_r,
    s_rs_s, s_rs_r, s_ag_s, s_ag_r, g_rs_s, g_rs_r, g_ag_s, g_ag_r, r_s, r_r, t_s, t_r,
):
    d = lax.axis_index("dp")
    s = lax.axis_index("seq")
    y = d // 16
    z = (d // 2) % 8
    c = d % 2
    p = (s // 4) % 2
    sib = (y * 16 + z * 2 + (1 - c), s)
    up = (y * 16 + ((z + 1) % 8) * 2 + c, s)
    down = (y * 16 + ((z + 7) % 8) * 2 + c, s)
    right = (d, (s + 4) % SEQ)
    left = (d, (s + 12) % SEQ)
    far_dp = (1 - y) * 16 + z * 2
    far_seq = s - 2 * (s % 4) + 3

    def remote(src, dst, ss, rs, dev):
        return pltpu.make_async_remote_copy(
            src_ref=src, dst_ref=dst, send_sem=ss, recv_sem=rs,
            device_id=dev, device_id_type=MESH,
        )

    def head(h):
        row = HEAD * h
        return pl.ds(row if isinstance(row, int) else pl.multiple_of(row, 16), HEAD)

    bases = (6 * c, 4 * (1 - c))

    def heads_of(i):
        return [bases[i] + n for n in range(GROUPS[i][0])]

    def rows_of(i, first, n):
        return pl.ds(pl.multiple_of(HEAD * bases[i] + first, 16), n)

    mine = pl.ds(0, ROWS)
    theirs = pl.ds(ROWS, ROWS)
    ins = [
        pltpu.make_async_copy(a, b, in_sem.at[i])
        for i, (a, b) in enumerate(
            (
                (k_in, k_raw), (q_in, q_raw), (og_in, og.at[pl.ds(0, MODEL), mine]),
                (w_in, w_raw.at[c]), (gq_in, gq_raw.at[c]), (gk_in, gk_raw.at[c]),
            )
        )
    ]
    ins_v = [
        pltpu.make_async_copy(v_in.at[head(h)], vx.at[h, pl.ds(0, HEAD)], v_sem.at[h])
        for h in range(HEADS)
    ]
    for cp in (ins[0], *ins_v, ins[1], ins[2]):
        cp.start()

    @pl.when(c == y)
    def _():
        for cp in ins[3:]:
            cp.start()

    bar = pltpu.get_barrier_semaphore()

    def greet_seq(o, u):
        pl.semaphore_signal(bar, inc=1, device_id=(d, (s + o) % SEQ), device_id_type=MESH)
        return u

    def greet(dev):
        pl.semaphore_signal(bar, inc=1, device_id=dev, device_id_type=MESH)

    lax.fori_loop(1, SEQ, greet_seq, 0)
    greet(sib)
    greet(up)
    greet(down)

    @pl.when(c != y)
    def _():
        greet((far_dp, far_seq))
        greet((far_dp + 1, far_seq))

    ones = jnp.where(iota((16, ROWS), 0) == 0, 1.0, 0.0).astype(BF)
    og[MODEL:, :] = jnp.zeros((2 * HALF - MODEL, 2 * ROWS), BF)
    acc[...] = jnp.zeros_like(acc)
    gacc[...] = jnp.zeros_like(gacc)

    def inverse(f):
        return lax.rsqrt(jnp.sum(f * f, axis=0, keepdims=True) * (1.0 / HEAD) + 1e-06)

    def piece_rows(g):
        return pl.ds(g[3], 16 * g[2])

    def rs_copy(i, sums, o, n):
        j = (s + o) % SEQ
        rows = rows_of(i, first_tile(GROUPS[i], j) * 16, 16 * n)
        piece = sums[1].at[o, pl.ds(GROUPS[i][3], 16 * n)]
        return remote(sums[0].at[rows], piece, sums[4].at[i, o], sums[5].at[i, o], (d, j))

    def ag_copy(i, sums, o, j, n):
        piece = sums[2].at[j, pl.ds(GROUPS[i][3], 16 * n)]
        return remote(piece, piece, sums[6].at[i, o], sums[7].at[i, o], (d, (s + o) % SEQ))

    def sized(i, j, act):
        g = GROUPS[i]
        owned = first_tile(g, j + 1) - first_tile(g, j)
        for n in (g[2] - 1, g[2]):
            pl.when(owned == n)(functools.partial(act, n))

    def each_peer(step):
        def body(o, u):
            step(o)
            return u

        lax.fori_loop(1, SEQ, body, 0)

    def rs_send(i, sums):
        each_peer(lambda o: sized(i, (s + o) % SEQ, lambda n: rs_copy(i, sums, o, n).start()))

    def rs_sum(i, sums):
        g = GROUPS[i]
        rows = rows_of(i, first_tile(g, s) * 16, 16 * g[2])

        def step(o, total):
            sized(i, s, lambda n: rs_copy(i, sums, o, n).wait_recv())
            return total + sums[1][o, g[3] : g[3] + 16 * g[2], :].astype(F32)

        return lax.fori_loop(1, SEQ, step, sums[0][rows, :].astype(F32))

    def ag_send(i, sums, total):
        g = GROUPS[i]
        sums[2][s, g[3] : g[3] + 16 * g[2], :] = total.astype(BF)
        each_peer(lambda o: sized(i, s, lambda n: ag_copy(i, sums, o, s, n).start()))

    def ag_wait(i, sums):
        g = GROUPS[i]

        def step(o):
            j = (s + SEQ - o) % SEQ
            sized(i, j, lambda n: ag_copy(i, sums, o, j, n).wait_recv())

        each_peer(step)
        for j in range(SEQ):
            n = 16 * OWNER[i].count(j)
            sums[3][rows_of(i, 16 * first_tile(g, j), n), :] = sums[2][j, g[3] : g[3] + n, :]

    s_sums = (s_loc, s_recv, s_all, s_full, s_rs_s, s_rs_r, s_ag_s, s_ag_r)
    g_sums = (g_loc, g_recv, g_all, g_full, g_rs_s, g_rs_r, g_ag_s, g_ag_r)

    def summary():
        ins[0].wait()
        for h in range(HEADS):
            ins_v[h].wait()
        vx[:, HEAD:, :] = jnp.broadcast_to(ones, (HEADS, PAD - HEAD, ROWS))
        for h in range(HEADS):
            kf = k_raw[head(h), :].astype(F32)
            r = inverse(kf)
            rk[h] = r
            phi = jnp.maximum(kf * r, 0.0).astype(BF)
            s_loc[head(h), :] = dot_nt(phi, vx[h]).astype(BF)

    early = z < 4

    @pl.when(early)
    def _():
        summary()

    pl.semaphore_wait(bar, SEQ - 1 + 4)

    def row_copies(kind, dev):
        return [
            remote(a, b.at[c], pair_s.at[kind, n], pair_r.at[c, n], dev)
            for n, (a, b) in enumerate(((w_in, w_raw), (gq_in, gq_raw), (gk_in, gk_raw)))
        ]

    far = row_copies(0, (far_dp + y, far_seq))
    near = row_copies(1, sib)
    for cp in far:
        cp.start()

    @pl.when(c != y)
    def _():
        for cp in near:
            cp.start()

    og_copy = remote(og_in, og.at[pl.ds(0, MODEL), theirs], misc_s.at[0], misc_r.at[0], sib)
    og_copy.start()

    @pl.when(early)
    def _():
        rs_send(0, s_sums)
        rs_send(1, s_sums)

    def wait_rows(i):
        for n, (a, b) in enumerate(((w_in, w_raw), (gq_in, gq_raw), (gk_in, gk_raw))):
            remote(a, b.at[i], pair_s.at[0, n], pair_r.at[i, n], sib).wait_recv()

    wait_rows(1 - c)

    @pl.when(c != y)
    def _():
        wait_rows(c)

    @pl.when(c == y)
    def _():
        for cp in ins[3:]:
            cp.wait()

    pair[...] = jnp.zeros_like(pair)
    diag = iota((48, OWN), 0) == iota((48, OWN), 1)
    lane = iota((48, 64), 1)
    for i in range(2):
        pair[i, 0:OWN, 0:MODEL] = w_raw[i]
        extra = jnp.zeros((48, 64), F32)
        for n, ref in enumerate((gq_raw, gk_raw)):
            rest = jnp.sum(
                jnp.where(diag, jnp.broadcast_to(ref[i], (48, OWN)), 0.0), axis=1, keepdims=True
            )
            for k in range(3):
                bits = rest.astype(BF).astype(F32)
                extra = jnp.where(lane == 3 * n + k, bits, extra)
                rest = rest - bits
        pair[i, :, MODEL:] = extra.astype(BF)
    m = iota((WIN, 96), 1)
    to = (70 * z) % 16 + jnp.where(m < 48, m, m - 13)
    to = jnp.where(to >= WIN, to - WIN, to)
    good = (m < OWN) | ((m >= 48) & (m < 48 + OWN))
    place = jnp.where((iota((WIN, 96), 0) == to) & good, 1.0, 0.0).astype(BF)
    both = pair[...].reshape(96, 2 * HALF)
    window = dot_nn(place, both).astype(BF)
    wbuf[0, z] = window[:, :HALF]
    wbuf[1, z] = window[:, HALF:]

    def part(e, b, q):
        return wbuf.at[e, b, :, pl.ds(CUT * q, CUT)]

    def z_copy(way, k, q):
        b = (z - (k - 1) + 8) % 8 if way == 0 else (z + (k - 1)) % 8
        ref = part(p, b, q)
        return remote(ref, ref, z_s.at[way, k - 1, q], z_r.at[way, k - 1, q], up if way == 0 else down)

    def x_copy(rel, q):
        ref = part(p, (z + rel) % 8, q)
        return remote(ref, ref, x_s.at[rel - 1, q], x_r.at[rel - 1, q], right if (q + rel) % 2 == 0 else left)

    def x_wait(rel):
        for q in range(PARTS):
            ref = part(1 - p, (z + rel) % 8, q)
            remote(ref, ref, x_s.at[rel - 1, q], x_r.at[rel - 1, q], right).wait_recv()

    def goes(way, k, q):
        return k < 4 or q % 2 == way

    def z_step(k):
        for q in range(PARTS):
            for way in range(2):
                if goes(way, k, q):
                    z_copy(way, k, q).wait_recv()
                    if k < 4 and goes(way, k + 1, q):
                        z_copy(way, k + 1, q).start()
                    x_copy(8 - k if way == 0 else k, q).start()

    for q in range(PARTS):
        z_copy(0, 1, q).start()
        z_copy(1, 1, q).start()

    @pl.when(z >= 4)
    def _():
        summary()
        rs_send(0, s_sums)
        rs_send(1, s_sums)

    row = iota((16, 1), 0)
    er = iota((128, 256), 0)
    el = iota((128, 256), 1)
    pick = ((er >= 64) & (er < 67) & (el < 128)) | ((er >= 67) & (er < 70) & (el >= 128))

    def add_rows(ref, b, res):
        start = pl.multiple_of(((70 * b) // 16) * 16, 16)
        phase = (70 * b) % 16
        over = phase + 70 - WIN
        ref[pl.ds(start, 16), :] += jnp.where(row >= phase, res[0:16], 0.0)
        ref[pl.ds(start + 16, WIN - 16), :] += res[16:]
        ref[pl.ds(start + WIN, 16), :] += jnp.where(row < over, res[0:16], 0.0)

    def product(e, b):
        rows = pl.ds(pl.multiple_of(e * HALF, 128), HALF)
        add_rows(acc, b, dot_nn(wbuf[e, b], og[rows, :]))
        spread = jnp.where(pick & (e == 1), 1.0, 0.0).astype(BF)
        add_rows(gacc, b, dot_nn(wbuf[e, b, :, HALF - 128 :], spread))

    ins[1].wait()
    for h in range(HEADS):
        rq[h] = inverse(q_raw[head(h), :].astype(F32))

    def spread_summary():
        for i in range(2):
            ag_send(i, s_sums, rs_sum(i, s_sums))

    @pl.when(early)
    def _():
        spread_summary()

    z_step(1)
    z_step(2)

    @pl.when(z >= 4)
    def _():
        spread_summary()

    ins[2].wait()
    og_copy.wait_recv()
    product(p, z)
    product(1 - p, z)
    z_step(3)
    for rel in (1, 7, 2, 6):
        product(p, (z + rel) % 8)
    z_step(4)
    ag_wait(0, s_sums)
    ag_wait(1, s_sums)
    for rel in (1, 7, 2, 6):
        x_wait(rel)
        product(1 - p, (z + rel) % 8)
    for rel in (3, 5, 4):
        product(p, (z + rel) % 8)
        x_wait(rel)
        product(1 - p, (z + rel) % 8)

    half_heads = 5 * HEAD
    att_send[...] = acc[0:half_heads, ROWS:].astype(BF)
    own_rows = pl.ds(pl.multiple_of(half_heads * c, 16), half_heads)
    other_rows = pl.ds(pl.multiple_of(half_heads * (1 - c), 16), half_heads)
    att_copy = remote(att_send, att.at[own_rows], misc_s.at[2], misc_r.at[2], sib)
    att_copy.start()
    gqk[own_rows, :] = gacc[0:half_heads, 0:128] * gacc[0:half_heads, 128:]
    gain_copy = remote(gqk.at[own_rows], gqk.at[own_rows], misc_s.at[1], misc_r.at[1], sib)
    gain_copy.start()
    att[own_rows, :] = acc[0:half_heads, 0:ROWS].astype(BF)

    def gain(h):
        g = gqk[head(h), :]
        return jnp.concatenate([g, g], axis=1)

    first = iota((16, ROWS), 0) == 0
    def grads_of(h):
        phi = jnp.maximum(q_raw[head(h), :].astype(F32) * rq[h], 0.0)
        num = dot_tn(s_full[head(h), :], (phi * gain(h)).astype(BF))
        inv = 1.0 / (num[HEAD : HEAD + 1] + float(TOKENS))
        ng = att[head(h), :].astype(F32) * inv
        dg = -jnp.sum(ng * num[0:HEAD], axis=0, keepdims=True) * inv
        ngx[h, 0:HEAD, :] = ng.astype(BF)
        ngx[h, HEAD:, :] = jnp.where(first, dg, 0.0).astype(BF)
        local = dot_nt(phi.astype(BF), ngx[h])
        g_loc[head(h), :] = local.astype(BF)
        sums = jnp.sum(local * s_full[head(h), :].astype(F32), axis=1, keepdims=True)
        i_col = HEAD * h + iota((HEAD, PAD), 0)
        spot = i_col - OWN * ((i_col * 1873) >> 16) == iota((HEAD, PAD), 1)
        spread = jnp.where(spot, jnp.broadcast_to(sums, (HEAD, PAD)), 0.0)
        i_row = HEAD * h + iota((DP, HEAD), 1)
        which = jnp.where((i_row * 1873) >> 16 == iota((DP, HEAD), 0), 1.0, 0.0).astype(BF)
        hi = spread.astype(BF)
        lo = (spread - hi.astype(F32)).astype(BF)
        return dot_nn(which, hi) + dot_nn(which, lo)

    wins = jnp.zeros((DP, PAD), F32)
    for h in heads_of(0):
        wins = wins + grads_of(h)
    rs_send(0, g_sums)
    remote(gqk.at[other_rows], gqk.at[other_rows], misc_s.at[1], misc_r.at[1], sib).wait_recv()
    remote(att_send, att.at[other_rows], misc_s.at[2], misc_r.at[2], sib).wait_recv()
    for h in heads_of(1):
        wins = wins + grads_of(h)
    rs_send(1, g_sums)
    win_send[...] = wins.reshape(DP, 1, PAD)

    def win_copy(o):
        e = (d + o) % DP
        return remote(win_send.at[e], win_recv.at[o], r_s.at[o], r_r.at[o], (e, s))

    def win_step(o, u):
        win_copy(o).start()
        return u

    lax.fori_loop(1, DP, win_step, 0)

    def norm_back(raw, r, grad):
        f = raw.astype(F32)
        a = jnp.where(f > 0, grad, 0.0)
        hat = f * r
        mean = jnp.sum(a * hat, axis=0, keepdims=True) * (1.0 / HEAD)
        return (r * (a - hat * mean)).astype(BF)

    def query_grad(h):
        g = dot_nn(s_full[head(h), :], ngx[h]) * gain(h)
        qg[head(h), :] = norm_back(q_raw[head(h), :], rq[h], g)

    for h in range(HEADS):
        query_grad(h)
    outs = [pltpu.make_async_copy(qg, qg_out, out_sem.at[0])]
    outs[0].start()

    for i in range(2):
        ag_send(i, g_sums, rs_sum(i, g_sums))

    def win_sum(o, total):
        win_copy(o).wait_recv()
        return total + win_recv[o]

    part_send[...] = lax.fori_loop(1, DP, win_sum, win_send[d])

    def part_copy(o):
        return remote(part_send, part_recv.at[o], t_s.at[o], t_r.at[o], (d, (s + o) % SEQ))

    def part_step(o, u):
        part_copy(o).start()
        return u

    lax.fori_loop(1, SEQ, part_step, 0)
    def key_grad(h):
        gg = gain(h)
        kf = k_raw[head(h), :].astype(F32)
        g = dot_nn(g_full[head(h), :], vx[h]) * gg
        kg[head(h), :] = norm_back(k_raw[head(h), :], rk[h], g)
        phi = (jnp.maximum(kf * rk[h], 0.0) * gg).astype(BF)
        vg[head(h), :] = dot_tn(g_full[head(h), :], phi)[0:HEAD].astype(BF)

    for i in range(2):
        ag_wait(i, g_sums)
        for h in heads_of(i):
            key_grad(h)
        rows = rows_of(i, 0, HEAD * GROUPS[i][0])
        for n, (a, b) in enumerate(((kg, kg_out), (vg, vg_out))):
            outs.append(pltpu.make_async_copy(a.at[rows], b.at[rows], out_sem.at[1 + 2 * i + n]))
            outs[-1].start()

    def part_sum(o, total):
        part_copy(o).wait_recv()
        return total + part_recv[o]

    total = lax.fori_loop(1, SEQ, part_sum, part_send[...])
    total_out[...] = total[:, 0:OWN]

    for cp in outs:
        cp.wait()
    for cp in far:
        cp.wait_send()

    @pl.when(c != y)
    def _():
        for cp in near:
            cp.wait_send()

    og_copy.wait_send()
    gain_copy.wait_send()
    att_copy.wait_send()
    for q in range(PARTS):
        for way in range(2):
            for k in range(1, 5):
                if goes(way, k, q):
                    z_copy(way, k, q).wait_send()
        for rel in range(1, 8):
            x_copy(rel, q).wait_send()

    def sent(o, u):
        for i in range(2):
            for sums in (s_sums, g_sums):
                sized(i, (s + o) % SEQ, lambda n: rs_copy(i, sums, o, n).wait_send())
                sized(i, s, lambda n: ag_copy(i, sums, o, s, n).wait_send())
        return u

    lax.fori_loop(1, SEQ, sent, 0)

    def win_sent(o, u):
        win_copy(o).wait_send()
        return u

    lax.fori_loop(1, DP, win_sent, 0)

    def part_sent(o, u):
        part_copy(o).wait_send()
        return u

    lax.fori_loop(1, SEQ, part_sent, 0)


def hand_over(qg_in, kg_in, vg_in, qg_out, kg_out, vg_out):
    qg_out[...] = qg_in[...]
    kg_out[...] = kg_in[...]
    vg_out[...] = vg_in[...]


def local(out_grad, out_weight, queries, keys, values, query_gain, key_norm_gain):
    V = pltpu.VMEM
    dma = pltpu.SemaphoreType.DMA
    any_, vm = pl.BlockSpec(memory_space=pl.ANY), pl.BlockSpec(memory_space=V)
    wide = jax.ShapeDtypeStruct((WIDTH, ROWS), BF)
    slim = jax.ShapeDtypeStruct((1, OWN), F32)
    summed = [
        V((WIDTH, PAD), BF), V((SEQ, PIECE, PAD), BF), V((SEQ, PIECE, PAD), BF), V((WIDTH, PAD), BF),
    ]
    outs = pl.pallas_call(
        kernel,
        out_shape=(wide, wide, wide, slim),
        in_specs=[any_] * 7,
        out_specs=(any_,) * 3 + (vm,),
        scratch_shapes=[
            V((2, 1, OWN), F32), V((2, 1, OWN), F32), *[V((WIDTH, ROWS), BF)] * 5, V((HEADS, PAD, ROWS), BF),
            V((2, OWN, MODEL), BF), V((2 * HALF, 2 * ROWS), BF),
            V((HEADS, 1, ROWS), F32), V((HEADS, 1, ROWS), F32), V((HEADS, PAD, ROWS), BF),
            V((2, 48, 2 * HALF), BF), V((2, 8, WIN, HALF), BF),
            V((5 * HEAD + 32, 2 * ROWS), F32), V((5 * HEAD + 32, 256), F32),
            V((WIDTH, ROWS), BF), V((5 * HEAD, ROWS), BF), V((WIDTH, PAD), F32),
            *summed, *summed,
            V((DP, 1, PAD), F32), V((DP, 1, PAD), F32), V((1, PAD), F32), V((SEQ, 1, PAD), F32),
            dma((6,)), dma((5,)), dma((HEADS,)), dma((3,)), dma((3,)), dma((2, 3)), dma((2, 3)),
            dma((2, 4, PARTS)), dma((2, 4, PARTS)), dma((7, PARTS)), dma((7, PARTS)),
            *[dma((2, SEQ))] * 8,
            dma((DP,)), dma((DP,)), dma((SEQ,)), dma((SEQ,)),
        ],
        compiler_params=pltpu.CompilerParams(
            collective_id=0, has_side_effects=True, vmem_limit_bytes=63 * 1024 * 1024
        ),
        cost_estimate=pl.CostEstimate(
            flops=2 * 512 * 2304 * 640, bytes_accessed=5_000_000, transcendentals=10_000
        ),
        name="attention_backward",
    )(
        out_grad[0].T, out_weight, queries[0].T, keys[0].T, values[0].T,
        query_gain.reshape(1, OWN), key_norm_gain.reshape(1, OWN),
    )
    qg, kg, vg, total = outs
    total = total.reshape(OWN)
    block = pl.BlockSpec((560, ROWS), lambda i: (i, 0))
    qg, kg, vg = pl.pallas_call(
        hand_over,
        grid=(2,),
        out_shape=(wide, wide, wide),
        in_specs=[block] * 3,
        out_specs=(block,) * 3,
        name="hand_over",
    )(qg, kg, vg)
    return qg.T[None], kg.T[None], vg.T[None], total * key_norm_gain, total * query_gain


def solution(mesh):
    placed = (
        P("dp", "seq", None),
        P("dp", None),
        P("dp", "seq", None),
        P("dp", "seq", None),
        P("dp", "seq", None),
        P("dp"),
        P("dp"),
    )
    return jax.shard_map(
        local,
        mesh=mesh,
        in_specs=placed,
        out_specs=(
            P("dp", "seq", None),
            P("dp", "seq", None),
            P("dp", "seq", None),
            P("dp"),
            P("dp"),
        ),
        check_vma=False,
    )
```

```python
import functools

import jax
import jax.numpy as jnp
from jax import lax
from jax.experimental import pallas as pl
from jax.experimental.pallas import tpu as pltpu
from jax.sharding import PartitionSpec as P

HEADS = 10
HEAD = 112
PAD = 128
ROWS = 256
WIDTH = HEADS * HEAD
MODEL = 2240
TOKENS = 4096
SEQ = 16
DP = 32
OWN = 35
HALF = 1152
CUT = 384
PARTS = HALF // CUT
WIN = 80
PIECE = 80
GROUPS = ((4, 28, 2, 0), (6, 42, 3, 32))
BF = jnp.bfloat16
F32 = jnp.float32
MESH = pl.DeviceIdType.MESH


def first_tile(group, j):
    return (group[1] * j) // SEQ


OWNER = [
    [max(j for j in range(SEQ) if first_tile(g, j) <= t) for t in range(g[1])] for g in GROUPS
]


def iota(shape, axis):
    return lax.broadcasted_iota(jnp.int32, shape, axis)


def dot_nt(a, b):
    return lax.dot_general(a, b, (((1,), (1,)), ((), ())), preferred_element_type=F32)


def dot_tn(a, b):
    return lax.dot_general(a, b, (((0,), (0,)), ((), ())), preferred_element_type=F32)


def dot_nn(a, b):
    return lax.dot_general(a, b, (((1,), (0,)), ((), ())), preferred_element_type=F32)


def kernel(
    og_in, w_in, q_in, k_in, v_in, gq_in, gk_in,
    qg_out, kg_out, vg_out, total_out,
    gq_raw, gk_raw, qg, kg, vg, k_raw, q_raw, vx, w_raw, og, rk, rq, ngx,
    pair, wbuf, acc, gacc, att, att_send, gqk,
    s_loc, s_recv, s_all, s_full,
    g_loc, g_recv, g_all, g_full,
    win_send, win_recv, part_send, part_recv,
    in_sem, out_sem, v_sem, misc_s, misc_r, pair_s, pair_r, z_s, z_r, x_s, x_r,
    s_rs_s, s_rs_r, s_ag_s, s_ag_r, g_rs_s, g_rs_r, g_ag_s, g_ag_r, r_s, r_r, t_s, t_r,
):
    d = lax.axis_index("dp")
    s = lax.axis_index("seq")
    y = d // 16
    z = (d // 2) % 8
    c = d % 2
    p = (s // 4) % 2
    sib = (y * 16 + z * 2 + (1 - c), s)
    up = (y * 16 + ((z + 1) % 8) * 2 + c, s)
    down = (y * 16 + ((z + 7) % 8) * 2 + c, s)
    right = (d, (s + 4) % SEQ)
    left = (d, (s + 12) % SEQ)
    far_dp = (1 - y) * 16 + z * 2
    far_seq = s - 2 * (s % 4) + 3

    def remote(src, dst, ss, rs, dev):
        return pltpu.make_async_remote_copy(
            src_ref=src, dst_ref=dst, send_sem=ss, recv_sem=rs,
            device_id=dev, device_id_type=MESH,
        )

    def head(h):
        row = HEAD * h
        return pl.ds(row if isinstance(row, int) else pl.multiple_of(row, 16), HEAD)

    bases = (6 * c, 4 * (1 - c))

    def heads_of(i):
        return [bases[i] + n for n in range(GROUPS[i][0])]

    def rows_of(i, first, n):
        return pl.ds(pl.multiple_of(HEAD * bases[i] + first, 16), n)

    mine = pl.ds(0, ROWS)
    theirs = pl.ds(ROWS, ROWS)
    ins = [
        pltpu.make_async_copy(a, b, in_sem.at[i])
        for i, (a, b) in enumerate(
            (
                (k_in, k_raw), (q_in, q_raw), (og_in, og.at[pl.ds(0, MODEL), mine]),
                (w_in, w_raw.at[c]), (gq_in, gq_raw.at[c]), (gk_in, gk_raw.at[c]),
            )
        )
    ]
    ins_v = [
        pltpu.make_async_copy(v_in.at[head(h)], vx.at[h, pl.ds(0, HEAD)], v_sem.at[h])
        for h in range(HEADS)
    ]
    for cp in (ins[0], *ins_v, ins[1], ins[2]):
        cp.start()

    @pl.when(c == y)
    def _():
        for cp in ins[3:]:
            cp.start()

    bar = pltpu.get_barrier_semaphore()

    def greet_seq(o, u):
        pl.semaphore_signal(bar, inc=1, device_id=(d, (s + o) % SEQ), device_id_type=MESH)
        return u

    def greet(dev):
        pl.semaphore_signal(bar, inc=1, device_id=dev, device_id_type=MESH)

    lax.fori_loop(1, SEQ, greet_seq, 0)
    greet(sib)
    greet(up)
    greet(down)

    @pl.when(c != y)
    def _():
        greet((far_dp, far_seq))
        greet((far_dp + 1, far_seq))

    ones = jnp.where(iota((16, ROWS), 0) == 0, 1.0, 0.0).astype(BF)
    og[MODEL:, :] = jnp.zeros((2 * HALF - MODEL, 2 * ROWS), BF)
    acc[...] = jnp.zeros_like(acc)
    gacc[...] = jnp.zeros_like(gacc)

    def inverse(f):
        return lax.rsqrt(jnp.sum(f * f, axis=0, keepdims=True) * (1.0 / HEAD) + 1e-06)

    def piece_rows(g):
        return pl.ds(g[3], 16 * g[2])

    def rs_copy(i, sums, o, n):
        j = (s + o) % SEQ
        rows = rows_of(i, first_tile(GROUPS[i], j) * 16, 16 * n)
        piece = sums[1].at[o, pl.ds(GROUPS[i][3], 16 * n)]
        return remote(sums[0].at[rows], piece, sums[4].at[i, o], sums[5].at[i, o], (d, j))

    def ag_copy(i, sums, o, j, n):
        piece = sums[2].at[j, pl.ds(GROUPS[i][3], 16 * n)]
        return remote(piece, piece, sums[6].at[i, o], sums[7].at[i, o], (d, (s + o) % SEQ))

    def sized(i, j, act):
        g = GROUPS[i]
        owned = first_tile(g, j + 1) - first_tile(g, j)
        for n in (g[2] - 1, g[2]):
            pl.when(owned == n)(functools.partial(act, n))

    def each_peer(step):
        def body(o, u):
            step(o)
            return u

        lax.fori_loop(1, SEQ, body, 0)

    def rs_send(i, sums):
        each_peer(lambda o: sized(i, (s + o) % SEQ, lambda n: rs_copy(i, sums, o, n).start()))

    def rs_sum(i, sums):
        g = GROUPS[i]
        rows = rows_of(i, first_tile(g, s) * 16, 16 * g[2])

        def step(o, total):
            sized(i, s, lambda n: rs_copy(i, sums, o, n).wait_recv())
            return total + sums[1][o, g[3] : g[3] + 16 * g[2], :].astype(F32)

        return lax.fori_loop(1, SEQ, step, sums[0][rows, :].astype(F32))

    def ag_send(i, sums, total):
        g = GROUPS[i]
        sums[2][s, g[3] : g[3] + 16 * g[2], :] = total.astype(BF)
        each_peer(lambda o: sized(i, s, lambda n: ag_copy(i, sums, o, s, n).start()))

    def ag_wait(i, sums):
        g = GROUPS[i]

        def step(o):
            j = (s + SEQ - o) % SEQ
            sized(i, j, lambda n: ag_copy(i, sums, o, j, n).wait_recv())

        each_peer(step)
        for j in range(SEQ):
            n = 16 * OWNER[i].count(j)
            sums[3][rows_of(i, 16 * first_tile(g, j), n), :] = sums[2][j, g[3] : g[3] + n, :]

    s_sums = (s_loc, s_recv, s_all, s_full, s_rs_s, s_rs_r, s_ag_s, s_ag_r)
    g_sums = (g_loc, g_recv, g_all, g_full, g_rs_s, g_rs_r, g_ag_s, g_ag_r)

    def summary():
        ins[0].wait()
        for h in range(HEADS):
            ins_v[h].wait()
        vx[:, HEAD:, :] = jnp.broadcast_to(ones, (HEADS, PAD - HEAD, ROWS))
        for h in range(HEADS):
            kf = k_raw[head(h), :].astype(F32)
            r = inverse(kf)
            rk[h] = r
            phi = jnp.maximum(kf * r, 0.0).astype(BF)
            s_loc[head(h), :] = dot_nt(phi, vx[h]).astype(BF)

    early = z < 4

    @pl.when(early)
    def _():
        summary()

    pl.semaphore_wait(bar, SEQ - 1 + 4)

    def row_copy(kind, i, dev, e=None):
        cols = pl.ds(0, MODEL) if e is None else pl.ds(HALF * e, (HALF, MODEL - HALF)[e])
        src, dst = (w_in, w_raw.at[i]) if e is None else (w_in.at[:, cols], w_raw.at[i, :, cols])
        return remote(src, dst, pair_s.at[kind, 0], pair_r.at[i, 0], dev)

    def gain_copies(kind, i, dev):
        return [
            remote(a, b.at[i], pair_s.at[kind, n], pair_r.at[i, n], dev)
            for n, a, b in ((1, gq_in, gq_raw), (2, gk_in, gk_raw))
        ]

    def by_half(act):
        for e in range(2):
            pl.when(p == e)(functools.partial(act, e))

    far_dev = (far_dp + y, far_seq)
    by_half(lambda e: row_copy(0, c, far_dev, e).start())
    for cp in gain_copies(0, c, far_dev):
        cp.start()

    @pl.when(c != y)
    def _():
        for cp in (row_copy(1, c, sib), *gain_copies(1, c, sib)):
            cp.start()

    og_copy = remote(og_in, og.at[pl.ds(0, MODEL), theirs], misc_s.at[0], misc_r.at[0], sib)
    og_copy.start()

    @pl.when(early)
    def _():
        rs_send(0, s_sums)
        rs_send(1, s_sums)

    @pl.when(c != y)
    def _():
        for i in range(2):
            by_half(lambda e: row_copy(0, i, sib, e).wait_recv())
            for cp in gain_copies(0, i, sib):
                cp.wait_recv()

    @pl.when(c == y)
    def _():
        for cp in (row_copy(0, 1 - c, sib), *gain_copies(0, 1 - c, sib)):
            cp.wait_recv()
        for cp in ins[3:]:
            cp.wait()

    pair[...] = jnp.zeros_like(pair)
    diag = iota((48, OWN), 0) == iota((48, OWN), 1)
    lane = iota((48, 64), 1)
    for i in range(2):
        pair[i, 0:OWN, 0:MODEL] = w_raw[i]
        extra = jnp.zeros((48, 64), F32)
        for n, ref in enumerate((gq_raw, gk_raw)):
            rest = jnp.sum(
                jnp.where(diag, jnp.broadcast_to(ref[i], (48, OWN)), 0.0), axis=1, keepdims=True
            )
            for k in range(3):
                bits = rest.astype(BF).astype(F32)
                extra = jnp.where(lane == 3 * n + k, bits, extra)
                rest = rest - bits
        pair[i, :, MODEL:] = extra.astype(BF)
    m = iota((WIN, 96), 1)
    to = (70 * z) % 16 + jnp.where(m < 48, m, m - 13)
    to = jnp.where(to >= WIN, to - WIN, to)
    good = (m < OWN) | ((m >= 48) & (m < 48 + OWN))
    place = jnp.where((iota((WIN, 96), 0) == to) & good, 1.0, 0.0).astype(BF)
    both = pair[...].reshape(96, 2 * HALF)
    window = dot_nn(place, both).astype(BF)
    for e in range(2):

        @pl.when((p == e) | (c == y))
        def _():
            wbuf[e, z] = window[:, HALF * e : HALF * (e + 1)]

    def part(e, b, q):
        return wbuf.at[e, b, :, pl.ds(CUT * q, CUT)]

    def z_copy(way, k, q):
        b = (z - (k - 1) + 8) % 8 if way == 0 else (z + (k - 1)) % 8
        ref = part(p, b, q)
        return remote(ref, ref, z_s.at[way, k - 1, q], z_r.at[way, k - 1, q], up if way == 0 else down)

    def x_copy(rel, q):
        ref = part(p, (z + rel) % 8, q)
        return remote(ref, ref, x_s.at[rel, q], x_r.at[rel, q], right if (q + rel) % 2 == 0 else left)

    def x_wait(rel):
        for q in range(PARTS):
            ref = part(1 - p, (z + rel) % 8, q)
            remote(ref, ref, x_s.at[rel, q], x_r.at[rel, q], right).wait_recv()

    def goes(way, k, q):
        return k < 4 or q % 2 == way

    def z_step(k):
        for q in range(PARTS):
            for way in range(2):
                if goes(way, k, q):
                    z_copy(way, k, q).wait_recv()
                    if k < 4 and goes(way, k + 1, q):
                        z_copy(way, k + 1, q).start()
                    x_copy(8 - k if way == 0 else k, q).start()

    for q in range(PARTS):
        z_copy(0, 1, q).start()
        z_copy(1, 1, q).start()

    @pl.when(c != y)
    def _():
        for q in range(PARTS):
            x_copy(0, q).start()

    @pl.when(z >= 4)
    def _():
        summary()
        rs_send(0, s_sums)
        rs_send(1, s_sums)

    row = iota((16, 1), 0)
    er = iota((128, 256), 0)
    el = iota((128, 256), 1)
    pick = ((er >= 64) & (er < 67) & (el < 128)) | ((er >= 67) & (er < 70) & (el >= 128))

    def add_rows(ref, b, res):
        start = pl.multiple_of(((70 * b) // 16) * 16, 16)
        phase = (70 * b) % 16
        over = phase + 70 - WIN
        ref[pl.ds(start, 16), :] += jnp.where(row >= phase, res[0:16], 0.0)
        ref[pl.ds(start + 16, WIN - 16), :] += res[16:]
        ref[pl.ds(start + WIN, 16), :] += jnp.where(row < over, res[0:16], 0.0)

    def product(e, b):
        rows = pl.ds(pl.multiple_of(e * HALF, 128), HALF)
        add_rows(acc, b, dot_nn(wbuf[e, b], og[rows, :]))
        spread = jnp.where(pick & (e == 1), 1.0, 0.0).astype(BF)
        add_rows(gacc, b, dot_nn(wbuf[e, b, :, HALF - 128 :], spread))

    ins[1].wait()
    for h in range(HEADS):
        rq[h] = inverse(q_raw[head(h), :].astype(F32))

    def spread_summary():
        for i in range(2):
            ag_send(i, s_sums, rs_sum(i, s_sums))

    @pl.when(early)
    def _():
        spread_summary()

    z_step(1)
    z_step(2)

    @pl.when(z >= 4)
    def _():
        spread_summary()

    ins[2].wait()
    og_copy.wait_recv()
    product(p, z)
    z_step(3)
    for rel in (1, 7, 2, 6):
        product(p, (z + rel) % 8)
    z_step(4)
    ag_wait(0, s_sums)
    ag_wait(1, s_sums)
    @pl.when(c != y)
    def _():
        x_wait(0)

    product(1 - p, z)
    for rel in (1, 7, 2, 6):
        x_wait(rel)
        product(1 - p, (z + rel) % 8)
    for rel in (3, 5, 4):
        product(p, (z + rel) % 8)
        x_wait(rel)
        product(1 - p, (z + rel) % 8)

    half_heads = 5 * HEAD
    att_send[...] = acc[0:half_heads, ROWS:].astype(BF)
    own_rows = pl.ds(pl.multiple_of(half_heads * c, 16), half_heads)
    other_rows = pl.ds(pl.multiple_of(half_heads * (1 - c), 16), half_heads)
    att_copy = remote(att_send, att.at[own_rows], misc_s.at[2], misc_r.at[2], sib)
    att_copy.start()
    gqk[own_rows, :] = gacc[0:half_heads, 0:128] * gacc[0:half_heads, 128:]
    gain_copy = remote(gqk.at[own_rows], gqk.at[own_rows], misc_s.at[1], misc_r.at[1], sib)
    gain_copy.start()
    att[own_rows, :] = acc[0:half_heads, 0:ROWS].astype(BF)

    def gain(h):
        g = gqk[head(h), :]
        return jnp.concatenate([g, g], axis=1)

    first = iota((16, ROWS), 0) == 0
    def grads_of(h):
        phi = jnp.maximum(q_raw[head(h), :].astype(F32) * rq[h], 0.0)
        num = dot_tn(s_full[head(h), :], (phi * gain(h)).astype(BF))
        inv = 1.0 / (num[HEAD : HEAD + 1] + float(TOKENS))
        ng = att[head(h), :].astype(F32) * inv
        dg = -jnp.sum(ng * num[0:HEAD], axis=0, keepdims=True) * inv
        ngx[h, 0:HEAD, :] = ng.astype(BF)
        ngx[h, HEAD:, :] = jnp.where(first, dg, 0.0).astype(BF)
        local = dot_nt(phi.astype(BF), ngx[h])
        g_loc[head(h), :] = local.astype(BF)
        sums = jnp.sum(local * s_full[head(h), :].astype(F32), axis=1, keepdims=True)
        i_col = HEAD * h + iota((HEAD, PAD), 0)
        spot = i_col - OWN * ((i_col * 1873) >> 16) == iota((HEAD, PAD), 1)
        spread = jnp.where(spot, jnp.broadcast_to(sums, (HEAD, PAD)), 0.0)
        i_row = HEAD * h + iota((DP, HEAD), 1)
        which = jnp.where((i_row * 1873) >> 16 == iota((DP, HEAD), 0), 1.0, 0.0).astype(BF)
        hi = spread.astype(BF)
        lo = (spread - hi.astype(F32)).astype(BF)
        return dot_nn(which, hi) + dot_nn(which, lo)

    wins = jnp.zeros((DP, PAD), F32)
    for h in heads_of(0):
        wins = wins + grads_of(h)
    rs_send(0, g_sums)
    remote(gqk.at[other_rows], gqk.at[other_rows], misc_s.at[1], misc_r.at[1], sib).wait_recv()
    remote(att_send, att.at[other_rows], misc_s.at[2], misc_r.at[2], sib).wait_recv()
    for h in heads_of(1):
        wins = wins + grads_of(h)
    rs_send(1, g_sums)
    win_send[...] = wins.reshape(DP, 1, PAD)

    def win_copy(o):
        e = (d + o) % DP
        return remote(win_send.at[e], win_recv.at[o], r_s.at[o], r_r.at[o], (e, s))

    def win_step(o, u):
        win_copy(o).start()
        return u

    lax.fori_loop(1, DP, win_step, 0)

    def norm_back(raw, r, grad):
        f = raw.astype(F32)
        a = jnp.where(f > 0, grad, 0.0)
        hat = f * r
        mean = jnp.sum(a * hat, axis=0, keepdims=True) * (1.0 / HEAD)
        return (r * (a - hat * mean)).astype(BF)

    def query_grad(h):
        g = dot_nn(s_full[head(h), :], ngx[h]) * gain(h)
        qg[head(h), :] = norm_back(q_raw[head(h), :], rq[h], g)

    for h in range(HEADS):
        query_grad(h)
    outs = [pltpu.make_async_copy(qg, qg_out, out_sem.at[0])]
    outs[0].start()

    for i in range(2):
        ag_send(i, g_sums, rs_sum(i, g_sums))

    def win_sum(o, total):
        win_copy(o).wait_recv()
        return total + win_recv[o]

    part_send[...] = lax.fori_loop(1, DP, win_sum, win_send[d])

    def part_copy(o):
        return remote(part_send, part_recv.at[o], t_s.at[o], t_r.at[o], (d, (s + o) % SEQ))

    def part_step(o, u):
        part_copy(o).start()
        return u

    lax.fori_loop(1, SEQ, part_step, 0)
    def key_grad(h):
        gg = gain(h)
        kf = k_raw[head(h), :].astype(F32)
        g = dot_nn(g_full[head(h), :], vx[h]) * gg
        kg[head(h), :] = norm_back(k_raw[head(h), :], rk[h], g)
        phi = (jnp.maximum(kf * rk[h], 0.0) * gg).astype(BF)
        vg[head(h), :] = dot_tn(g_full[head(h), :], phi)[0:HEAD].astype(BF)

    for i in range(2):
        ag_wait(i, g_sums)
        for h in heads_of(i):
            key_grad(h)
        rows = rows_of(i, 0, HEAD * GROUPS[i][0])
        for n, (a, b) in enumerate(((kg, kg_out), (vg, vg_out))):
            outs.append(pltpu.make_async_copy(a.at[rows], b.at[rows], out_sem.at[1 + 2 * i + n]))
            outs[-1].start()

    def part_sum(o, total):
        part_copy(o).wait_recv()
        return total + part_recv[o]

    total = lax.fori_loop(1, SEQ, part_sum, part_send[...])
    total_out[...] = total[:, 0:OWN]

    for cp in outs:
        cp.wait()
    by_half(lambda e: row_copy(0, c, far_dev, e).wait_send())
    for cp in gain_copies(0, c, far_dev):
        cp.wait_send()

    @pl.when(c != y)
    def _():
        for cp in (row_copy(1, c, sib), *gain_copies(1, c, sib)):
            cp.wait_send()
        for q in range(PARTS):
            x_copy(0, q).wait_send()

    og_copy.wait_send()
    gain_copy.wait_send()
    att_copy.wait_send()
    for q in range(PARTS):
        for way in range(2):
            for k in range(1, 5):
                if goes(way, k, q):
                    z_copy(way, k, q).wait_send()
        for rel in range(1, 8):
            x_copy(rel, q).wait_send()

    def sent(o, u):
        for i in range(2):
            for sums in (s_sums, g_sums):
                sized(i, (s + o) % SEQ, lambda n: rs_copy(i, sums, o, n).wait_send())
                sized(i, s, lambda n: ag_copy(i, sums, o, s, n).wait_send())
        return u

    lax.fori_loop(1, SEQ, sent, 0)

    def win_sent(o, u):
        win_copy(o).wait_send()
        return u

    lax.fori_loop(1, DP, win_sent, 0)

    def part_sent(o, u):
        part_copy(o).wait_send()
        return u

    lax.fori_loop(1, SEQ, part_sent, 0)


def hand_over(qg_in, kg_in, vg_in, qg_out, kg_out, vg_out):
    qg_out[...] = qg_in[...]
    kg_out[...] = kg_in[...]
    vg_out[...] = vg_in[...]


def local(out_grad, out_weight, queries, keys, values, query_gain, key_norm_gain):
    V = pltpu.VMEM
    dma = pltpu.SemaphoreType.DMA
    any_, vm = pl.BlockSpec(memory_space=pl.ANY), pl.BlockSpec(memory_space=V)
    wide = jax.ShapeDtypeStruct((WIDTH, ROWS), BF)
    slim = jax.ShapeDtypeStruct((1, OWN), F32)
    summed = [
        V((WIDTH, PAD), BF), V((SEQ, PIECE, PAD), BF), V((SEQ, PIECE, PAD), BF), V((WIDTH, PAD), BF),
    ]
    outs = pl.pallas_call(
        kernel,
        out_shape=(wide, wide, wide, slim),
        in_specs=[any_] * 7,
        out_specs=(any_,) * 3 + (vm,),
        scratch_shapes=[
            V((2, 1, OWN), F32), V((2, 1, OWN), F32), *[V((WIDTH, ROWS), BF)] * 5, V((HEADS, PAD, ROWS), BF),
            V((2, OWN, MODEL), BF), V((2 * HALF, 2 * ROWS), BF),
            V((HEADS, 1, ROWS), F32), V((HEADS, 1, ROWS), F32), V((HEADS, PAD, ROWS), BF),
            V((2, 48, 2 * HALF), BF), V((2, 8, WIN, HALF), BF),
            V((5 * HEAD + 32, 2 * ROWS), F32), V((5 * HEAD + 32, 256), F32),
            V((WIDTH, ROWS), BF), V((5 * HEAD, ROWS), BF), V((WIDTH, PAD), F32),
            *summed, *summed,
            V((DP, 1, PAD), F32), V((DP, 1, PAD), F32), V((1, PAD), F32), V((SEQ, 1, PAD), F32),
            dma((6,)), dma((5,)), dma((HEADS,)), dma((3,)), dma((3,)), dma((2, 3)), dma((2, 3)),
            dma((2, 4, PARTS)), dma((2, 4, PARTS)), dma((8, PARTS)), dma((8, PARTS)),
            *[dma((2, SEQ))] * 8,
            dma((DP,)), dma((DP,)), dma((SEQ,)), dma((SEQ,)),
        ],
        compiler_params=pltpu.CompilerParams(
            collective_id=0, has_side_effects=True, vmem_limit_bytes=63 * 1024 * 1024
        ),
        cost_estimate=pl.CostEstimate(
            flops=2 * 512 * 2304 * 640, bytes_accessed=5_000_000, transcendentals=10_000
        ),
        name="attention_backward",
    )(
        out_grad[0].T, out_weight, queries[0].T, keys[0].T, values[0].T,
        query_gain.reshape(1, OWN), key_norm_gain.reshape(1, OWN),
    )
    qg, kg, vg, total = outs
    total = total.reshape(OWN)
    block = pl.BlockSpec((560, ROWS), lambda i: (i, 0))
    qg, kg, vg = pl.pallas_call(
        hand_over,
        grid=(2,),
        out_shape=(wide, wide, wide),
        in_specs=[block] * 3,
        out_specs=(block,) * 3,
        name="hand_over",
    )(qg, kg, vg)
    return qg.T[None], kg.T[None], vg.T[None], total * key_norm_gain, total * query_gain


def solution(mesh):
    placed = (
        P("dp", "seq", None),
        P("dp", None),
        P("dp", "seq", None),
        P("dp", "seq", None),
        P("dp", "seq", None),
        P("dp"),
        P("dp"),
    )
    return jax.shard_map(
        local,
        mesh=mesh,
        in_specs=placed,
        out_specs=(
            P("dp", "seq", None),
            P("dp", "seq", None),
            P("dp", "seq", None),
            P("dp"),
            P("dp"),
        ),
        check_vma=False,
    )
```

```python
import functools

import jax
import jax.numpy as jnp
from jax import lax
from jax.experimental import pallas as pl
from jax.experimental.pallas import tpu as pltpu
from jax.sharding import PartitionSpec as P

HEADS = 10
HEAD = 112
PAD = 128
ROWS = 256
WIDTH = HEADS * HEAD
MODEL = 2240
TOKENS = 4096
SEQ = 16
DP = 32
OWN = 35
HALF = 1152
CUT = 384
PARTS = HALF // CUT
WIN = 80
PIECE = 80
GROUPS = ((4, 28, 2, 0), (6, 42, 3, 32))
BF = jnp.bfloat16
F32 = jnp.float32
MESH = pl.DeviceIdType.MESH


def first_tile(group, j):
    return (group[1] * j) // SEQ


OWNER = [
    [max(j for j in range(SEQ) if first_tile(g, j) <= t) for t in range(g[1])] for g in GROUPS
]


def iota(shape, axis):
    return lax.broadcasted_iota(jnp.int32, shape, axis)


def dot_nt(a, b):
    return lax.dot_general(a, b, (((1,), (1,)), ((), ())), preferred_element_type=F32)


def dot_tn(a, b):
    return lax.dot_general(a, b, (((0,), (0,)), ((), ())), preferred_element_type=F32)


def dot_nn(a, b):
    return lax.dot_general(a, b, (((1,), (0,)), ((), ())), preferred_element_type=F32)


def kernel(
    og_in, w_in, q_in, k_in, v_in, gq_in, gk_in,
    qg_out, kg_out, vg_out, total_out,
    gq_raw, gk_raw, qg, kg, vg, k_raw, q_raw, vx, w_raw, og, rk, rq, ngx,
    pair, wbuf, acc, gacc, att, att_send, gqk,
    s_loc, s_recv, s_all, s_full,
    g_loc, g_recv, g_all, g_full,
    g_wide, win_send, win_recv, part_send, part_recv,
    in_sem, out_sem, v_sem, misc_s, misc_r, pair_s, pair_r, z_s, z_r, x_s, x_r,
    s_rs_s, s_rs_r, s_ag_s, s_ag_r, g_rs_s, g_rs_r, g_ag_s, g_ag_r, r_s, r_r, t_s, t_r,
):
    d = lax.axis_index("dp")
    s = lax.axis_index("seq")
    y = d // 16
    z = (d // 2) % 8
    c = d % 2
    p = (s // 4) % 2
    sib = (y * 16 + z * 2 + (1 - c), s)
    up = (y * 16 + ((z + 1) % 8) * 2 + c, s)
    down = (y * 16 + ((z + 7) % 8) * 2 + c, s)
    right = (d, (s + 4) % SEQ)
    left = (d, (s + 12) % SEQ)
    far_dp = (1 - y) * 16 + z * 2
    far_seq = s - 2 * (s % 4) + 3

    def remote(src, dst, ss, rs, dev):
        return pltpu.make_async_remote_copy(
            src_ref=src, dst_ref=dst, send_sem=ss, recv_sem=rs,
            device_id=dev, device_id_type=MESH,
        )

    def head(h):
        row = HEAD * h
        return pl.ds(row if isinstance(row, int) else pl.multiple_of(row, 16), HEAD)

    bases = (6 * c, 4 * (1 - c))

    def heads_of(i):
        return [bases[i] + n for n in range(GROUPS[i][0])]

    def rows_of(i, first, n):
        return pl.ds(pl.multiple_of(HEAD * bases[i] + first, 16), n)

    mine = pl.ds(0, ROWS)
    theirs = pl.ds(ROWS, ROWS)
    ins = [
        pltpu.make_async_copy(a, b, in_sem.at[i])
        for i, (a, b) in enumerate(
            (
                (k_in, k_raw), (q_in, q_raw), (og_in, og.at[pl.ds(0, MODEL), mine]),
                (w_in, w_raw.at[c]), (gq_in, gq_raw.at[c]), (gk_in, gk_raw.at[c]),
            )
        )
    ]
    ins_v = [
        pltpu.make_async_copy(v_in.at[head(h)], vx.at[h, pl.ds(0, HEAD)], v_sem.at[h])
        for h in range(HEADS)
    ]
    for cp in (ins[0], *ins_v, ins[1], ins[2]):
        cp.start()

    @pl.when(c == y)
    def _():
        for cp in ins[3:]:
            cp.start()

    bar = pltpu.get_barrier_semaphore()

    def greet_seq(o, u):
        pl.semaphore_signal(bar, inc=1, device_id=(d, (s + o) % SEQ), device_id_type=MESH)
        return u

    def greet(dev):
        pl.semaphore_signal(bar, inc=1, device_id=dev, device_id_type=MESH)

    lax.fori_loop(1, SEQ, greet_seq, 0)
    greet(sib)
    greet(up)
    greet(down)

    @pl.when(c != y)
    def _():
        greet((far_dp, far_seq))
        greet((far_dp + 1, far_seq))

    ones = jnp.where(iota((16, ROWS), 0) == 0, 1.0, 0.0).astype(BF)
    og[MODEL:, :] = jnp.zeros((2 * HALF - MODEL, 2 * ROWS), BF)
    acc[...] = jnp.zeros_like(acc)
    gacc[...] = jnp.zeros_like(gacc)

    def inverse(f):
        return lax.rsqrt(jnp.sum(f * f, axis=0, keepdims=True) * (1.0 / HEAD) + 1e-06)

    def piece_rows(g):
        return pl.ds(g[3], 16 * g[2])

    def rs_copy(i, sums, o, n):
        j = (s + o) % SEQ
        rows = rows_of(i, first_tile(GROUPS[i], j) * 16, 16 * n)
        piece = sums[1].at[o, pl.ds(GROUPS[i][3], 16 * n)]
        return remote(sums[0].at[rows], piece, sums[4].at[i, o], sums[5].at[i, o], (d, j))

    def ag_copy(i, sums, o, j, n):
        piece = sums[2].at[j, pl.ds(GROUPS[i][3], 16 * n)]
        return remote(piece, piece, sums[6].at[i, o], sums[7].at[i, o], (d, (s + o) % SEQ))

    def sized(i, j, act):
        g = GROUPS[i]
        owned = first_tile(g, j + 1) - first_tile(g, j)
        for n in (g[2] - 1, g[2]):
            pl.when(owned == n)(functools.partial(act, n))

    def each_peer(step):
        def body(o, u):
            step(o)
            return u

        lax.fori_loop(1, SEQ, body, 0)

    def rs_send(i, sums):
        each_peer(lambda o: sized(i, (s + o) % SEQ, lambda n: rs_copy(i, sums, o, n).start()))

    def rs_sum(i, sums):
        g = GROUPS[i]
        rows = rows_of(i, first_tile(g, s) * 16, 16 * g[2])

        def step(o, total):
            sized(i, s, lambda n: rs_copy(i, sums, o, n).wait_recv())
            return total + sums[1][o, g[3] : g[3] + 16 * g[2], :].astype(F32)

        return lax.fori_loop(1, SEQ, step, sums[0][rows, :].astype(F32))

    def ag_send(i, sums, total):
        g = GROUPS[i]
        sums[2][s, g[3] : g[3] + 16 * g[2], :] = total.astype(BF)
        each_peer(lambda o: sized(i, s, lambda n: ag_copy(i, sums, o, s, n).start()))

    def ag_wait(i, sums):
        g = GROUPS[i]

        def step(o):
            j = (s + SEQ - o) % SEQ
            sized(i, j, lambda n: ag_copy(i, sums, o, j, n).wait_recv())

        each_peer(step)
        for j in range(SEQ):
            n = 16 * OWNER[i].count(j)
            sums[3][rows_of(i, 16 * first_tile(g, j), n), :] = sums[2][j, g[3] : g[3] + n, :]

    s_sums = (s_loc, s_recv, s_all, s_full, s_rs_s, s_rs_r, s_ag_s, s_ag_r)
    g_sums = (g_loc, g_recv, g_all, g_full, g_rs_s, g_rs_r, g_ag_s, g_ag_r)

    def summary():
        ins[0].wait()
        for h in range(HEADS):
            ins_v[h].wait()
        vx[:, HEAD:, :] = jnp.broadcast_to(ones, (HEADS, PAD - HEAD, ROWS))
        for h in range(HEADS):
            kf = k_raw[head(h), :].astype(F32)
            r = inverse(kf)
            rk[h] = r
            phi = jnp.maximum(kf * r, 0.0).astype(BF)
            s_loc[head(h), :] = dot_nt(phi, vx[h]).astype(BF)

    early = z < 4

    @pl.when(early)
    def _():
        summary()

    pl.semaphore_wait(bar, SEQ - 1 + 4)

    def row_copy(kind, i, dev, e=None):
        cols = pl.ds(0, MODEL) if e is None else pl.ds(HALF * e, (HALF, MODEL - HALF)[e])
        src, dst = (w_in, w_raw.at[i]) if e is None else (w_in.at[:, cols], w_raw.at[i, :, cols])
        return remote(src, dst, pair_s.at[kind, 0], pair_r.at[i, 0], dev)

    def gain_copies(kind, i, dev):
        return [
            remote(a, b.at[i], pair_s.at[kind, n], pair_r.at[i, n], dev)
            for n, a, b in ((1, gq_in, gq_raw), (2, gk_in, gk_raw))
        ]

    def by_half(act):
        for e in range(2):
            pl.when(p == e)(functools.partial(act, e))

    far_dev = (far_dp + y, far_seq)
    by_half(lambda e: row_copy(0, c, far_dev, e).start())
    for cp in gain_copies(0, c, far_dev):
        cp.start()

    @pl.when(c != y)
    def _():
        for cp in (row_copy(1, c, sib), *gain_copies(1, c, sib)):
            cp.start()

    og_copy = remote(og_in, og.at[pl.ds(0, MODEL), theirs], misc_s.at[0], misc_r.at[0], sib)
    og_copy.start()

    @pl.when(early)
    def _():
        rs_send(0, s_sums)
        rs_send(1, s_sums)

    @pl.when(c != y)
    def _():
        for i in range(2):
            by_half(lambda e: row_copy(0, i, sib, e).wait_recv())
            for cp in gain_copies(0, i, sib):
                cp.wait_recv()

    @pl.when(c == y)
    def _():
        for cp in (row_copy(0, 1 - c, sib), *gain_copies(0, 1 - c, sib)):
            cp.wait_recv()
        for cp in ins[3:]:
            cp.wait()

    pair[...] = jnp.zeros_like(pair)
    diag = iota((48, OWN), 0) == iota((48, OWN), 1)
    lane = iota((48, 64), 1)
    for i in range(2):
        pair[i, 0:OWN, 0:MODEL] = w_raw[i]
        extra = jnp.zeros((48, 64), F32)
        for n, ref in enumerate((gq_raw, gk_raw)):
            rest = jnp.sum(
                jnp.where(diag, jnp.broadcast_to(ref[i], (48, OWN)), 0.0), axis=1, keepdims=True
            )
            for k in range(3):
                bits = rest.astype(BF).astype(F32)
                extra = jnp.where(lane == 3 * n + k, bits, extra)
                rest = rest - bits
        pair[i, :, MODEL:] = extra.astype(BF)
    m = iota((WIN, 96), 1)
    to = (70 * z) % 16 + jnp.where(m < 48, m, m - 13)
    to = jnp.where(to >= WIN, to - WIN, to)
    good = (m < OWN) | ((m >= 48) & (m < 48 + OWN))
    place = jnp.where((iota((WIN, 96), 0) == to) & good, 1.0, 0.0).astype(BF)
    both = pair[...].reshape(96, 2 * HALF)
    window = dot_nn(place, both).astype(BF)
    for e in range(2):

        @pl.when((p == e) | (c == y))
        def _():
            wbuf[e, z] = window[:, HALF * e : HALF * (e + 1)]

    def part(e, b, q):
        return wbuf.at[e, b, :, pl.ds(CUT * q, CUT)]

    def z_copy(way, k, q):
        b = (z - (k - 1) + 8) % 8 if way == 0 else (z + (k - 1)) % 8
        ref = part(p, b, q)
        return remote(ref, ref, z_s.at[way, k - 1, q], z_r.at[way, k - 1, q], up if way == 0 else down)

    def x_copy(rel, q):
        ref = part(p, (z + rel) % 8, q)
        return remote(ref, ref, x_s.at[rel, q], x_r.at[rel, q], right if (q + rel) % 2 == 0 else left)

    def x_wait(rel):
        for q in range(PARTS):
            ref = part(1 - p, (z + rel) % 8, q)
            remote(ref, ref, x_s.at[rel, q], x_r.at[rel, q], right).wait_recv()

    def goes(way, k, q):
        return k < 4 or q % 2 == way

    def z_step(k):
        for q in range(PARTS):
            for way in range(2):
                if goes(way, k, q):
                    z_copy(way, k, q).wait_recv()
                    if k < 4 and goes(way, k + 1, q):
                        z_copy(way, k + 1, q).start()
                    x_copy(8 - k if way == 0 else k, q).start()

    for q in range(PARTS):
        z_copy(0, 1, q).start()
        z_copy(1, 1, q).start()

    @pl.when(c != y)
    def _():
        for q in range(PARTS):
            x_copy(0, q).start()

    @pl.when(z >= 4)
    def _():
        summary()
        rs_send(0, s_sums)
        rs_send(1, s_sums)

    row = iota((16, 1), 0)
    er = iota((128, 256), 0)
    el = iota((128, 256), 1)
    pick = ((er >= 64) & (er < 67) & (el < 128)) | ((er >= 67) & (er < 70) & (el >= 128))

    def add_rows(ref, b, res):
        start = pl.multiple_of(((70 * b) // 16) * 16, 16)
        phase = (70 * b) % 16
        over = phase + 70 - WIN
        ref[pl.ds(start, 16), :] += jnp.where(row >= phase, res[0:16], 0.0)
        ref[pl.ds(start + 16, WIN - 16), :] += res[16:]
        ref[pl.ds(start + WIN, 16), :] += jnp.where(row < over, res[0:16], 0.0)

    def product(e, b):
        rows = pl.ds(pl.multiple_of(e * HALF, 128), HALF)
        add_rows(acc, b, dot_nn(wbuf[e, b], og[rows, :]))
        spread = jnp.where(pick & (e == 1), 1.0, 0.0).astype(BF)
        add_rows(gacc, b, dot_nn(wbuf[e, b, :, HALF - 128 :], spread))

    ins[1].wait()
    for h in range(HEADS):
        rq[h] = inverse(q_raw[head(h), :].astype(F32))

    def spread_summary():
        for i in range(2):
            ag_send(i, s_sums, rs_sum(i, s_sums))

    @pl.when(early)
    def _():
        spread_summary()

    z_step(1)
    z_step(2)

    @pl.when(z >= 4)
    def _():
        spread_summary()

    ins[2].wait()
    og_copy.wait_recv()
    product(p, z)
    z_step(3)
    for rel in (1, 7, 2, 6):
        product(p, (z + rel) % 8)
    z_step(4)
    ag_wait(0, s_sums)
    ag_wait(1, s_sums)
    @pl.when(c != y)
    def _():
        x_wait(0)

    product(1 - p, z)
    for rel in (1, 7, 2, 6):
        x_wait(rel)
        product(1 - p, (z + rel) % 8)
    for rel in (3, 5, 4):
        product(p, (z + rel) % 8)
        x_wait(rel)
        product(1 - p, (z + rel) % 8)

    half_heads = 5 * HEAD
    att_send[...] = acc[0:half_heads, ROWS:].astype(BF)
    own_rows = pl.ds(pl.multiple_of(half_heads * c, 16), half_heads)
    other_rows = pl.ds(pl.multiple_of(half_heads * (1 - c), 16), half_heads)
    att_copy = remote(att_send, att.at[own_rows], misc_s.at[2], misc_r.at[2], sib)
    att_copy.start()
    gqk[own_rows, :] = gacc[0:half_heads, 0:128] * gacc[0:half_heads, 128:]
    gain_copy = remote(gqk.at[own_rows], gqk.at[own_rows], misc_s.at[1], misc_r.at[1], sib)
    gain_copy.start()
    att[own_rows, :] = acc[0:half_heads, 0:ROWS].astype(BF)

    def gain(h):
        g = gqk[head(h), :]
        return jnp.concatenate([g, g], axis=1)

    first = iota((16, ROWS), 0) == 0
    def grads_of(h):
        phi = jnp.maximum(q_raw[head(h), :].astype(F32) * rq[h], 0.0)
        num = dot_tn(s_full[head(h), :], (phi * gain(h)).astype(BF))
        inv = 1.0 / (num[HEAD : HEAD + 1] + float(TOKENS))
        ng = att[head(h), :].astype(F32) * inv
        dg = -jnp.sum(ng * num[0:HEAD], axis=0, keepdims=True) * inv
        ngx[h, 0:HEAD, :] = ng.astype(BF)
        ngx[h, HEAD:, :] = jnp.where(first, dg, 0.0).astype(BF)
        local = dot_nt(phi.astype(BF), ngx[h])
        g_wide[head(h), :] = local
        g_loc[head(h), :] = local.astype(BF)

    def windows_of(h):
        sums = jnp.sum(g_wide[head(h), :] * s_full[head(h), :].astype(F32), axis=1, keepdims=True)
        i_col = HEAD * h + iota((HEAD, PAD), 0)
        spot = i_col - OWN * ((i_col * 1873) >> 16) == iota((HEAD, PAD), 1)
        spread = jnp.where(spot, jnp.broadcast_to(sums, (HEAD, PAD)), 0.0)
        i_row = HEAD * h + iota((DP, HEAD), 1)
        which = jnp.where((i_row * 1873) >> 16 == iota((DP, HEAD), 0), 1.0, 0.0).astype(BF)
        hi = spread.astype(BF)
        lo = (spread - hi.astype(F32)).astype(BF)
        return dot_nn(which, hi) + dot_nn(which, lo)

    for h in heads_of(0):
        grads_of(h)
    rs_send(0, g_sums)
    remote(gqk.at[other_rows], gqk.at[other_rows], misc_s.at[1], misc_r.at[1], sib).wait_recv()
    remote(att_send, att.at[other_rows], misc_s.at[2], misc_r.at[2], sib).wait_recv()
    for h in heads_of(1):
        grads_of(h)
    rs_send(1, g_sums)
    wins = jnp.zeros((DP, PAD), F32)
    for h in range(HEADS):
        wins = wins + windows_of(h)
    win_send[...] = wins.reshape(DP, 1, PAD)

    def win_copy(o):
        e = (d + o) % DP
        return remote(win_send.at[e], win_recv.at[o], r_s.at[o], r_r.at[o], (e, s))

    def win_step(o, u):
        win_copy(o).start()
        return u

    lax.fori_loop(1, DP, win_step, 0)

    def norm_back(raw, r, grad):
        f = raw.astype(F32)
        a = jnp.where(f > 0, grad, 0.0)
        hat = f * r
        mean = jnp.sum(a * hat, axis=0, keepdims=True) * (1.0 / HEAD)
        return (r * (a - hat * mean)).astype(BF)

    def query_grad(h):
        g = dot_nn(s_full[head(h), :], ngx[h]) * gain(h)
        qg[head(h), :] = norm_back(q_raw[head(h), :], rq[h], g)

    for h in range(HEADS):
        query_grad(h)
    outs = [pltpu.make_async_copy(qg, qg_out, out_sem.at[0])]
    outs[0].start()

    for i in range(2):
        ag_send(i, g_sums, rs_sum(i, g_sums))

    def win_sum(o, total):
        win_copy(o).wait_recv()
        return total + win_recv[o]

    part_send[...] = lax.fori_loop(1, DP, win_sum, win_send[d])

    def part_copy(o):
        return remote(part_send, part_recv.at[o], t_s.at[o], t_r.at[o], (d, (s + o) % SEQ))

    def part_step(o, u):
        part_copy(o).start()
        return u

    lax.fori_loop(1, SEQ, part_step, 0)
    def key_grad(h):
        gg = gain(h)
        kf = k_raw[head(h), :].astype(F32)
        g = dot_nn(g_full[head(h), :], vx[h]) * gg
        kg[head(h), :] = norm_back(k_raw[head(h), :], rk[h], g)
        phi = (jnp.maximum(kf * rk[h], 0.0) * gg).astype(BF)
        vg[head(h), :] = dot_tn(g_full[head(h), :], phi)[0:HEAD].astype(BF)

    for i in range(2):
        ag_wait(i, g_sums)
        for h in heads_of(i):
            key_grad(h)
        rows = rows_of(i, 0, HEAD * GROUPS[i][0])
        for n, (a, b) in enumerate(((kg, kg_out), (vg, vg_out))):
            outs.append(pltpu.make_async_copy(a.at[rows], b.at[rows], out_sem.at[1 + 2 * i + n]))
            outs[-1].start()

    def part_sum(o, total):
        part_copy(o).wait_recv()
        return total + part_recv[o]

    total = lax.fori_loop(1, SEQ, part_sum, part_send[...])
    total_out[...] = total[:, 0:OWN]

    for cp in outs:
        cp.wait()
    by_half(lambda e: row_copy(0, c, far_dev, e).wait_send())
    for cp in gain_copies(0, c, far_dev):
        cp.wait_send()

    @pl.when(c != y)
    def _():
        for cp in (row_copy(1, c, sib), *gain_copies(1, c, sib)):
            cp.wait_send()
        for q in range(PARTS):
            x_copy(0, q).wait_send()

    og_copy.wait_send()
    gain_copy.wait_send()
    att_copy.wait_send()
    for q in range(PARTS):
        for way in range(2):
            for k in range(1, 5):
                if goes(way, k, q):
                    z_copy(way, k, q).wait_send()
        for rel in range(1, 8):
            x_copy(rel, q).wait_send()

    def sent(o, u):
        for i in range(2):
            for sums in (s_sums, g_sums):
                sized(i, (s + o) % SEQ, lambda n: rs_copy(i, sums, o, n).wait_send())
                sized(i, s, lambda n: ag_copy(i, sums, o, s, n).wait_send())
        return u

    lax.fori_loop(1, SEQ, sent, 0)

    def win_sent(o, u):
        win_copy(o).wait_send()
        return u

    lax.fori_loop(1, DP, win_sent, 0)

    def part_sent(o, u):
        part_copy(o).wait_send()
        return u

    lax.fori_loop(1, SEQ, part_sent, 0)


def hand_over(qg_in, kg_in, vg_in, qg_out, kg_out, vg_out):
    qg_out[...] = qg_in[...]
    kg_out[...] = kg_in[...]
    vg_out[...] = vg_in[...]


def local(out_grad, out_weight, queries, keys, values, query_gain, key_norm_gain):
    V = pltpu.VMEM
    dma = pltpu.SemaphoreType.DMA
    any_, vm = pl.BlockSpec(memory_space=pl.ANY), pl.BlockSpec(memory_space=V)
    wide = jax.ShapeDtypeStruct((WIDTH, ROWS), BF)
    slim = jax.ShapeDtypeStruct((1, OWN), F32)
    summed = [
        V((WIDTH, PAD), BF), V((SEQ, PIECE, PAD), BF), V((SEQ, PIECE, PAD), BF), V((WIDTH, PAD), BF),
    ]
    outs = pl.pallas_call(
        kernel,
        out_shape=(wide, wide, wide, slim),
        in_specs=[any_] * 7,
        out_specs=(any_,) * 3 + (vm,),
        scratch_shapes=[
            V((2, 1, OWN), F32), V((2, 1, OWN), F32), *[V((WIDTH, ROWS), BF)] * 5, V((HEADS, PAD, ROWS), BF),
            V((2, OWN, MODEL), BF), V((2 * HALF, 2 * ROWS), BF),
            V((HEADS, 1, ROWS), F32), V((HEADS, 1, ROWS), F32), V((HEADS, PAD, ROWS), BF),
            V((2, 48, 2 * HALF), BF), V((2, 8, WIN, HALF), BF),
            V((5 * HEAD + 32, 2 * ROWS), F32), V((5 * HEAD + 32, 256), F32),
            V((WIDTH, ROWS), BF), V((5 * HEAD, ROWS), BF), V((WIDTH, PAD), F32),
            *summed, *summed,
            V((WIDTH, PAD), F32), V((DP, 1, PAD), F32), V((DP, 1, PAD), F32), V((1, PAD), F32), V((SEQ, 1, PAD), F32),
            dma((6,)), dma((5,)), dma((HEADS,)), dma((3,)), dma((3,)), dma((2, 3)), dma((2, 3)),
            dma((2, 4, PARTS)), dma((2, 4, PARTS)), dma((8, PARTS)), dma((8, PARTS)),
            *[dma((2, SEQ))] * 8,
            dma((DP,)), dma((DP,)), dma((SEQ,)), dma((SEQ,)),
        ],
        compiler_params=pltpu.CompilerParams(
            collective_id=0, has_side_effects=True, vmem_limit_bytes=63 * 1024 * 1024
        ),
        cost_estimate=pl.CostEstimate(
            flops=2 * 512 * 2304 * 640, bytes_accessed=5_000_000, transcendentals=10_000
        ),
        name="attention_backward",
    )(
        out_grad[0].T, out_weight, queries[0].T, keys[0].T, values[0].T,
        query_gain.reshape(1, OWN), key_norm_gain.reshape(1, OWN),
    )
    qg, kg, vg, total = outs
    total = total.reshape(OWN)
    block = pl.BlockSpec((560, ROWS), lambda i: (i, 0))
    qg, kg, vg = pl.pallas_call(
        hand_over,
        grid=(2,),
        out_shape=(wide, wide, wide),
        in_specs=[block] * 3,
        out_specs=(block,) * 3,
        name="hand_over",
    )(qg, kg, vg)
    return qg.T[None], kg.T[None], vg.T[None], total * key_norm_gain, total * query_gain


def solution(mesh):
    placed = (
        P("dp", "seq", None),
        P("dp", None),
        P("dp", "seq", None),
        P("dp", "seq", None),
        P("dp", "seq", None),
        P("dp"),
        P("dp"),
    )
    return jax.shard_map(
        local,
        mesh=mesh,
        in_specs=placed,
        out_specs=(
            P("dp", "seq", None),
            P("dp", "seq", None),
            P("dp", "seq", None),
            P("dp"),
            P("dp"),
        ),
        check_vma=False,
    )
```
